768 devices in a mesh: tower: 24 (over z_lo, x, core), local: 32 (over y, z_hi).
Axes of the slice: x: 4, y: 8, z: 12 (z_hi: 4, z_lo: 3; z = z_hi * 3 + z_lo), core: 2. Of those that a mesh axis runs over, the one named last changes fastest.
Arguments:
- top_cot: bfloat16 [32, 384, 4096], P('local', 'tower'), may hold values from -6 to 6
- top_pre: bfloat16 [32, 384, 4096], P('local', 'tower'), may hold values from -6 to 6
- top_weight: bfloat16 [6144, 4096], P('tower'), may hold values from -0.078125 to 0.078125
- tower_pre: bfloat16 [32, 384, 6144], P('local', None, 'tower'), may hold values from -6 to 6
- tower_weight: bfloat16 [24, 1536, 256], P('tower'), may hold values from -0.15625 to 0.15625
- pooled: bfloat16 [32, 384, 24, 1536], P('local', None, 'tower'), may hold values from -6 to 6
- feature_ids: int32 [32, 384, 24, 12, 4], P('local', None, 'tower'), may hold values from 0 to 255
- bag_lengths: int32 [32, 384, 24, 12], P('local', None, 'tower'), may hold values from 1 to 4
- block_slot: int32 [96], replicated, may hold values from 0 to 95, each once
Outputs:
- top_grad: float32 [6144, 4096], P('tower', 'local')
- tower_grad: float32 [24, 1536, 256], P('tower', 'local')
- emb_grad: float32 [24, 96, 32, 128], P('tower', 'local')
The draws below stay inside these ranges and needn't reach their ends.
Inputs may be any that keep to these rules, and one draw needn't show every extreme that they name: block_slot is a permutation of the 96 slots.
All inputs are finite; a program needn't handle non-finite values.
Results may differ from the reference program's by a relative error of at most 0.015.
Values may be sent and summed in bfloat16 or wider, within the bound.
A program may use at most 64 MiB of HBM per device.

```python
import math
import jax
import jax.numpy as jnp
from jax import lax

TOPW = 4096
WOUT = 256
FEAT_T = 12
E = 128
BAG = 4
FROWS = 256
BLK = 32
TOWERS = 24
GROUPS = 32
GROUP = 384
SAMPLES = 12288
FEAT = 6144
SLAB = 1536
NBLK = 96


def set_ends(result, key, least, largest):
    spot = [jax.random.randint(jax.random.fold_in(key, axis), (), 0, length) for axis, length in enumerate(result.shape)]
    longest = result.shape.index(max(result.shape))
    next_to = spot[:longest] + [(spot[longest] + 1) % result.shape[longest]] + spot[longest + 1:]
    return result.at[tuple(spot)].set(least).at[tuple(next_to)].set(largest)


def strengthened(values, key, source, target, blocks, factor):
    owner, partner = [(jnp.arange(values.shape[position]) // (values.shape[position] // blocks)).reshape([-1 if axis == position else 1 for axis in range(values.ndim)]) for position in (source, target)]
    chosen = jax.random.permutation(key, blocks)[partner]
    strong = (owner == chosen) | (owner == (partner + blocks // 2) % blocks)
    return jnp.where(strong, factor * values, values)


def shard_levels(own_key, shape, split, least, top_value):
    gain, own = 1.0, jax.random.fold_in(own_key, 6)
    for axis_at, parts in split:
        steps = jnp.exp(jax.random.uniform(jax.random.fold_in(own, axis_at), (parts,), jnp.float32, least / len(split), top_value / len(split)))
        gain = gain * jnp.repeat(steps, shape[axis_at] // parts).reshape([-1 if axis == axis_at else 1 for axis in range(len(shape))])
    return gain


def scatter_about(rng, dims, deviation, limit, cuts=(), kind=jnp.bfloat16):
    drawn = deviation * jax.random.normal(rng, dims, jnp.float32)
    if cuts:
        drawn = drawn * shard_levels(rng, dims, cuts, -0.22, 0.18)
    return jnp.clip(drawn, -limit, limit).astype(kind)


def bell_draw_with(key, extent, spread, limit, split, heavy, kind=jnp.bfloat16):
    drawn = spread * jax.random.normal(key, extent, jnp.float32)
    if split:
        drawn = drawn * shard_levels(key, extent, split, -0.22, 0.18)
    return jnp.clip(strengthened(drawn, jax.random.fold_in(key, 3), *heavy), -limit, limit).astype(kind)


def setup_inputs(seed: int = 0) -> dict:
    seeds = jax.random.split(jax.random.key(seed), 10)
    top_cot = bell_draw_with(seeds[0], (GROUPS, GROUP, TOPW), 1.0, 6.0, ((0, 32), (1, 24)), (0, 2, 32, 2.75))
    top_pre = scatter_about(seeds[1], (GROUPS, GROUP, TOPW), 1.0, 6.0, ((0, 32), (1, 24)))
    top_weight = scatter_about(seeds[2], (FEAT, TOPW), FEAT ** -0.5, 0.078125, ((0, 24),))
    tower_pre = scatter_about(seeds[3], (GROUPS, GROUP, FEAT), 1.0, 6.0, ((0, 32), (2, 24)))
    tower_weight = scatter_about(seeds[4], (TOWERS, SLAB, WOUT), SLAB ** -0.5, 0.15625, ((0, 24),))
    pooled = scatter_about(seeds[5], (GROUPS, GROUP, TOWERS, SLAB), 1.0, 6.0, ((0, 32), (2, 24)))
    feature_ids = set_ends(jax.random.randint(seeds[6], (GROUPS, GROUP, TOWERS, FEAT_T, BAG), 0, FROWS), jax.random.fold_in(seeds[6], 1), 0, FROWS - 1).astype(jnp.int32)
    bag_lengths = set_ends(jax.random.randint(seeds[7], (GROUPS, GROUP, TOWERS, FEAT_T), 1, BAG + 1), jax.random.fold_in(seeds[7], 1), 1, BAG).astype(jnp.int32)
    block_slot = jax.random.permutation(seeds[8], NBLK).astype(jnp.int32)
    return {"top_cot": top_cot, "top_pre": top_pre, "top_weight": top_weight, "tower_pre": tower_pre, "tower_weight": tower_weight, "pooled": pooled, "feature_ids": feature_ids, "bag_lengths": bag_lengths, "block_slot": block_slot}


def gelu_value(values):
    return 0.5 * values * (1.0 + jax.scipy.special.erf(values / math.sqrt(2.0)))

def gelu_slope(values):
    return 0.5 * (1.0 + jax.scipy.special.erf(values / math.sqrt(2.0))) + values * jnp.exp(-0.5 * values * values) / math.sqrt(2.0 * math.pi)

def reference(top_cot, top_pre, top_weight, tower_pre, tower_weight, pooled, feature_ids, bag_lengths, block_slot):
    factor = 1.0 / math.sqrt(SAMPLES)
    delta = (top_cot.astype(jnp.float32) * gelu_slope(top_pre.astype(jnp.float32))).astype(jnp.bfloat16)
    flat = delta.reshape(SAMPLES, TOPW)
    feature_grad = jnp.dot(flat, top_weight.T, preferred_element_type=jnp.float32).astype(jnp.bfloat16)
    pre_flat = tower_pre.reshape(SAMPLES, FEAT).astype(jnp.float32)
    compressed = gelu_value(pre_flat).astype(jnp.bfloat16)
    top_grad = jnp.dot(compressed.T, flat, preferred_element_type=jnp.float32) * factor
    tower_delta = (feature_grad.astype(jnp.float32) * gelu_slope(pre_flat)).astype(jnp.bfloat16)
    tower_delta = tower_delta.reshape(SAMPLES, TOWERS, WOUT)
    pool_all = pooled.reshape(SAMPLES, TOWERS, SLAB)
    ids_all = feature_ids.reshape(SAMPLES, TOWERS, FEAT_T, BAG)
    lens_all = bag_lengths.reshape(SAMPLES, TOWERS, FEAT_T)

    def per_tower(index):
        delta_t = tower_delta[:, index]
        grad_t = jnp.dot(pool_all[:, index].T, delta_t, preferred_element_type=jnp.float32) * factor
        pooled_grad = jnp.dot(delta_t, tower_weight[index].T, preferred_element_type=jnp.float32).astype(jnp.bfloat16)
        pooled_grad = pooled_grad.reshape(SAMPLES, FEAT_T, E)
        rows = jnp.arange(FEAT_T, dtype=jnp.int32)[None, :, None] * FROWS + ids_all[:, index]
        valid = jnp.arange(BAG, dtype=jnp.int32)[None, None, :] < lens_all[:, index][:, :, None]
        values = jnp.where(valid[..., None], pooled_grad[:, :, None, :].astype(jnp.float32), jnp.float32(0.0))
        dense = jax.ops.segment_sum(values.reshape(-1, E), rows.reshape(-1), num_segments=FEAT_T * FROWS)
        blocks = dense.reshape(NBLK, BLK, E)
        slotted = jnp.zeros((NBLK, BLK, E), jnp.float32).at[block_slot].set(blocks)
        return (grad_t, slotted)
    tower_grad, emb_grad = lax.map(per_tower, jnp.arange(TOWERS, dtype=jnp.int32))
    return (top_grad, tower_grad, emb_grad)
```

```python
import math

import jax
import jax.numpy as jnp
from jax import lax
from jax.experimental import pallas as pl
from jax.experimental.pallas import tpu as pltpu
from jax.sharding import PartitionSpec as P

MESH = pl.DeviceIdType.MESH
F32, BF16 = jnp.float32, jnp.bfloat16

NZL, NX, NC, NY, NZH = 3, 4, 2, 8, 4
TOPW, WOUT, FEATS, EMB, BAG, FROWS, BLK = 4096, 256, 12, 128, 4, 256, 32
GROUP, SLAB, NBLK = 384, 1536, 96
SHARD = GROUP // (NZL * NX * NC)
LANES = TOPW // (NY * NZH)
PHASES = NZH
OFF = (2, 1, 3, 0)
WIDE = NY * LANES
HALF_WIDE = WIDE // 2
TOW_ROWS = SLAB // (NY * NZH)
EMB_ROWS = NBLK * BLK // (NY * NZH)
FACTOR = 1.0 / math.sqrt(12288)


def gelu_value(values):
    return 0.5 * values * (1.0 + lax.erf(values / math.sqrt(2.0)))


def gelu_slope(values):
    return 0.5 * (1.0 + lax.erf(values / math.sqrt(2.0))) + values * jnp.exp(
        -0.5 * values * values
    ) / math.sqrt(2.0 * math.pi)


def wide_sum(*terms):
    total = terms[0].astype(F32)
    for term in terms[1:]:
        total = total + term.astype(F32)
    return total


def kernel(
    cot_hbm, pre_hbm, tower_pre_hbm, ids_hbm, lens_hbm, slot_hbm, weight_hbm, tower_weight_hbm,
    pooled_hbm, out_top, out_tow, out_emb,
    cot, pre, tower_pre, ids, lens, slot, rows, weight, tower_weight, pooled, pooled_t, comp_t, slope, part, delta_t, counts, dense, slotted,
    top, tow, emb, rb_top, rb_tow, rb_emb,
    zs_top, zb_top, zf_top, zy_tow, zs_tow, zb_tow, zf_tow, zy_emb, zs_emb, zb_emb, zf_emb,
    load_sem, weight_sem, zl_send, zl_recv, x_send, x_recv, n_send, n_recv, b_send, b_recv,
    y_send, y_recv, zh_send, zh_recv,
):
    t, l = lax.axis_index("tower"), lax.axis_index("local")
    core, x, zl = lax.rem(t, NC), lax.rem(lax.div(t, NC), NX), lax.div(t, NC * NX)
    y, zh = lax.div(l, NZH), lax.rem(l, NZH)

    def at_tower(zl_, x_, core_):
        return ((zl_ * NX + x_) * NC + core_, l)

    def at_local(y_, zh_):
        return (t, y_ * NZH + zh_)

    xp, xm = lax.rem(x + 1, NX), lax.rem(x + NX - 1, NX)
    xo = lax.rem(x + 2, NX)
    zl_next = [lax.rem(zl + d, NZL) for d in (1, 2)]
    zl_prev = [lax.rem(zl + NZL - d, NZL) for d in (1, 2)]
    y_next = [lax.rem(y + 1, NY), lax.rem(y + NY - 1, NY)]
    zh_next = [lax.rem(zh + 1, NZH), lax.rem(zh + NZH - 1, NZH)]
    dev_zl = [at_tower(zl_, x, core) for zl_ in zl_next]
    dev_x = [at_tower(zl, x_, core) for x_ in (xp, xm)]
    dev_sib = at_tower(zl, x, 1 - core)
    dev_y = [at_local(y_, zh) for y_ in y_next]
    dev_zh = [at_local(y, zh_) for zh_ in zh_next]

    barrier = pltpu.get_barrier_semaphore()
    peers = dev_zl + dev_x + [dev_sib] + dev_y + dev_zh
    for peer in peers:
        pl.semaphore_signal(barrier, inc=1, device_id=peer, device_id_type=MESH)

    def first_column(q, k):
        owner = lax.rem(y + k, NY) * NZH + lax.rem(zh + OFF[q], NZH)
        return pl.multiple_of(owner * LANES, LANES)

    def remote(src, dst, send, recv, device):
        return pltpu.make_async_remote_copy(
            src_ref=src, dst_ref=dst, send_sem=send, recv_sem=recv,
            device_id=device, device_id_type=MESH,
        )

    loads = [
        pltpu.make_async_copy(src, dst, load_sem.at[i])
        for i, (src, dst) in enumerate(
            [
                (cot_hbm, cot), (pre_hbm, pre), (tower_pre_hbm, tower_pre), (ids_hbm, ids),
                (lens_hbm, lens), (slot_hbm, slot), (pooled_hbm, pooled),
                (tower_weight_hbm, tower_weight),
            ]
        )
    ]
    load_cot, load_pre, load_tower_pre, load_ids, load_lens, load_slot, load_pool, load_tw = loads
    for load in loads[:6]:
        load.start()
    for q in range(PHASES):
        for k in range(NY):
            pltpu.make_async_copy(
                weight_hbm.at[:, pl.ds(first_column(q, k), LANES)],
                weight.at[q, :, pl.ds(k * LANES, LANES)],
                weight_sem.at[q],
            ).start()
    load_pool.start()
    load_tw.start()
    load_cot.wait()
    load_pre.wait()

    for q in range(PHASES):
        for k in range(NY):
            cols = pl.ds(first_column(q, k), LANES)
            value = cot[:, cols].astype(F32) * gelu_slope(pre[:, cols].astype(F32))
            rows[q, zl, x, core, :, pl.ds(k * LANES, LANES)] = value.astype(BF16)

    pl.semaphore_wait(barrier, len(peers))

    def zl_copy(q, d):
        here = rows.at[q, zl, x, core]
        return remote(here, here, zl_send.at[q, d], zl_recv.at[q, d], dev_zl[d])

    def zl_arrival(q, d):
        there = rows.at[q, zl_prev[d], x, core]
        return remote(there, there, zl_send.at[q, d], zl_recv.at[q, d], dev_zl[1 - d])

    def x_copy(q, d):
        here = rows.at[q, :, x, core]
        return remote(here, here, x_send.at[q, d], x_recv.at[q, d], dev_x[d])

    def x_arrival(q, d):
        there = rows.at[q, :, (xm, xp)[d], core]
        return remote(there, there, x_send.at[q, d], x_recv.at[q, d], dev_x[1 - d])

    def n_copy(q, d):
        there = rows.at[q, :, (xm, xp)[d], core, :, pl.ds(d * HALF_WIDE, HALF_WIDE)]
        return remote(there, there, n_send.at[q, d], n_recv.at[q, d], dev_x[d])

    def n_arrival(q, d):
        there = rows.at[q, :, xo, core, :, pl.ds(d * HALF_WIDE, HALF_WIDE)]
        return remote(there, there, n_send.at[q, d], n_recv.at[q, d], dev_x[1 - d])

    def b_copy(q):
        here = rows.at[q, :, :, core]
        return remote(here, here, b_send.at[q], b_recv.at[q], dev_sib)

    def b_arrival(q):
        there = rows.at[q, :, :, 1 - core]
        return remote(there, there, b_send.at[q], b_recv.at[q], dev_sib)

    def step_z(q):
        for d in range(2):
            zl_copy(q, d).start()

    def step_x(q):
        for d in range(2):
            zl_arrival(q, d).wait_recv()
        for d in range(2):
            x_copy(q, d).start()

    def step_n(q):
        for d in range(2):
            x_arrival(q, d).wait_recv()
            n_copy(q, d).start()

    def step_b(q):
        for d in range(2):
            n_arrival(q, d).wait_recv()
        b_copy(q).start()

    half_rows = [WOUT // 2] * PHASES + [NZH * TOW_ROWS // 2, NZH * EMB_ROWS // 2]

    def chunk(p, k):
        if p < PHASES:
            return top.at[p, k]
        y_ = lax.rem(y + k, NY)
        if p == PHASES:
            return tow.at[pl.ds(pl.multiple_of(y_ * (NZH * TOW_ROWS), 16), NZH * TOW_ROWS)]
        return emb.at[pl.ds(pl.multiple_of(y_ * (NZH * EMB_ROWS), 16), NZH * EMB_ROWS)]

    def landing(p, d, h):
        ref = rb_top.at[p, d, h] if p < PHASES else (rb_tow, rb_emb)[p - PHASES].at[d, h]
        return ref.at[pl.ds(0, half_rows[p])] if h == 0 else ref

    def half(p, d):
        return pl.ds(d * half_rows[p], half_rows[p])

    def y_copy(p, d, h):
        if h == 0:
            src = chunk(p, NY // 2).at[half(p, d)]
        else:
            src = chunk(p, NY // 2 - h if d == 0 else NY // 2 + h)
        return remote(src, landing(p, d, h), y_send.at[p, d, h], y_recv.at[p, d, h], dev_y[d])

    def step_s(p):
        for d in range(2):
            y_copy(p, d, 0).start()

    def step_h(p, h):
        for d in range(2):
            y_copy(p, d, h - 1).wait_recv()
            own = chunk(p, NY // 2 - h if d == 0 else NY // 2 + h)
            if h == 1:
                own = own.at[half(p, d)]
            own[...] = wide_sum(own[...], landing(p, d, h - 1)[...]).astype(BF16)
            y_copy(p, d, h).start()

    def y_total(p):
        last = NY // 2 - 1
        for d in range(2):
            y_copy(p, d, last).wait_recv()
        return wide_sum(chunk(p, 0)[...], landing(p, 0, last)[...], landing(p, 1, last)[...])

    def zh_copy(i, src, dst, d):
        return remote(src, dst, zh_send.at[i], zh_recv.at[i], dev_zh[d])

    top_halves = [pl.ds(d * (WOUT // 2), WOUT // 2) for d in range(2)]
    zc_top = [zh_copy(d, zs_top.at[0, top_halves[d]], zb_top.at[d], d) for d in range(2)]
    zc_top += [zh_copy(2 + d, zs_top.at[1 + d], zf_top.at[d], d) for d in range(2)]
    zc_tow = [zh_copy(4, zs_tow.at[0], zb_tow, 0)]
    zc_tow += [zh_copy(5 + d, zs_tow.at[1 + d], zf_tow.at[d], d) for d in range(2)]
    zc_emb = [zh_copy(7, zs_emb.at[0], zb_emb, 1)]
    zc_emb += [zh_copy(8 + d, zs_emb.at[1 + d], zf_emb.at[d], d) for d in range(2)]

    def step_f_top(q):
        total = y_total(q)
        if q == 0:
            zs_top[0] = total.astype(BF16)
            for d in range(2):
                zc_top[d].start()
        elif q < 3:
            d = q - 1
            zc_top[d].wait_recv()
            zs_top[q] = total.astype(BF16)
            zs_top[q, top_halves[d]] = wide_sum(
                total[d * (WOUT // 2) : (d + 1) * (WOUT // 2)], zb_top[d]
            ).astype(BF16)
            zc_top[q + 1].start()
        else:
            out_top[...] = total

    def blocks(ref, size, offset):
        first = lax.rem(zh + offset, NZH) * size
        return ref[pl.ds(pl.multiple_of(first, 16), size), :]

    def step_f_pair(p, zy, zs, size, copies, via):
        zy[...] = y_total(p)
        zs[0] = blocks(zy, size, 2).astype(BF16)
        copies[0].start()
        zs[2 - via] = blocks(zy, size, (1, 3)[1 - via]).astype(BF16)
        copies[2 - via].start()

    def step_g_pair(zy, zs, zb, size, copies, via):
        copies[0].wait_recv()
        zs[1 + via] = wide_sum(blocks(zy, size, (1, 3)[via]), zb[...]).astype(BF16)
        copies[1 + via].start()

    def prepare_pre():
        load_tower_pre.wait()
        values = tower_pre[...].astype(F32)
        slope[...] = gelu_slope(values)
        comp_t[...] = gelu_value(values).T.astype(BF16)

    def prepare_counts(first, last):
        size = 64
        if first == 0:
            load_ids.wait()
            load_lens.wait()

        def feature(f, carry):
            length = lens[f]
            masked = [jnp.where(j < length, ids[f, j : j + 1, :], -1) for j in range(BAG)]
            for part_ in range(FROWS // size):
                table = lax.broadcasted_iota(jnp.int32, (size, GROUP), 0) + part_ * size
                hits = [jnp.where(m == table, 1.0, 0.0) for m in masked]
                count = (hits[0] + hits[1]) + (hits[2] + hits[3])
                counts[f, pl.ds(part_ * size, size), :] = count.astype(BF16)
            return carry

        lax.fori_loop(first, last, feature, 0)

    def prepare_pooled(first, last):
        if first == 0:
            load_pool.wait()
        for c in range(first, last):
            block = pooled[:, c * EMB : (c + 1) * EMB].astype(F32)
            pooled_t[c * EMB : (c + 1) * EMB, :] = block.T.astype(BF16)

    def compute_phase(q):
        b_arrival(q).wait_recv()
        pltpu.make_async_copy(weight.at[q], weight.at[q], weight_sem.at[q]).wait()
        for k in range(0, NY, 2):
            deltas = rows[q, :, :, :, :, k * LANES : (k + 2) * LANES].reshape(GROUP, 2 * LANES)
            term = jnp.dot(comp_t[...], deltas, preferred_element_type=F32) * FACTOR
            top[q, k] = term[:, :LANES].astype(BF16)
            top[q, k + 1] = term[:, LANES:].astype(BF16)
        step_s(q)
        deltas = rows[q].reshape(GROUP, WIDE)
        product = lax.dot_general(
            deltas, weight[q], (((1,), (1,)), ((), ())), preferred_element_type=F32
        )
        part[...] = product if q == 0 else part[...] + product

    def compute_tow():
        feature_grad = part[...].astype(BF16).astype(F32)
        delta_t[...] = (feature_grad * slope[...]).astype(BF16)
        for c in range(0, SLAB, 256):
            term = jnp.dot(pooled_t[c : c + 256, :], delta_t[...], preferred_element_type=F32)
            tow[c : c + 256, :] = (term * FACTOR).astype(BF16)

    def compute_emb():
        load_tw.wait()
        for f in range(FEATS):
            grad = lax.dot_general(
                delta_t[...], tower_weight[f * EMB : (f + 1) * EMB, :],
                (((1,), (1,)), ((), ())), preferred_element_type=F32,
            ).astype(BF16)
            dense[f * FROWS : (f + 1) * FROWS, :] = jnp.dot(
                counts[f], grad, preferred_element_type=F32
            )
        load_slot.wait()
        numbers = lax.broadcasted_iota(jnp.int32, (NBLK, NBLK), 0)
        moves = jnp.where(slot[...] == numbers, 1.0, 0.0).astype(BF16)
        for i in range(0, BLK, 2):
            taken = [dense[pl.ds(i + j, NBLK, stride=BLK), :].astype(BF16) for j in range(2)]
            moved = jnp.dot(moves, jnp.concatenate(taken, 1), preferred_element_type=F32)
            for j in range(2):
                slotted[pl.ds(i + j, NBLK, stride=BLK), :] = moved[:, j * EMB : (j + 1) * EMB]
        emb[...] = slotted[...].astype(BF16)

    for q in range(PHASES):
        step_z(q)
    prepare_pre()
    step_x(0)
    prepare_counts(0, 4)
    step_x(1)
    step_n(0)
    prepare_counts(4, 8)
    step_x(2)
    step_b(0)
    step_n(1)
    prepare_counts(8, 12)
    step_x(3)
    step_b(1)
    step_n(2)
    compute_phase(0)
    prepare_pooled(0, 6)
    step_b(2)
    step_n(3)
    compute_phase(1)
    step_h(0, 1)
    prepare_pooled(6, 12)
    step_b(3)
    compute_phase(2)
    step_h(0, 2)
    step_h(1, 1)
    compute_phase(3)
    step_h(0, 3)
    step_h(1, 2)
    step_h(2, 1)
    compute_tow()
    step_s(4)
    step_f_top(0)
    step_h(1, 3)
    step_h(2, 2)
    step_h(3, 1)
    compute_emb()
    step_s(5)
    step_f_top(1)
    step_h(2, 3)
    step_h(3, 2)
    step_h(4, 1)
    step_f_top(2)
    step_h(3, 3)
    step_h(4, 2)
    step_h(5, 1)
    step_f_top(3)
    step_h(4, 3)
    step_h(5, 2)
    step_f_pair(4, zy_tow, zs_tow, TOW_ROWS, zc_tow, 0)
    step_h(5, 3)
    step_g_pair(zy_tow, zs_tow, zb_tow, TOW_ROWS, zc_tow, 0)
    for d in range(2):
        zc_top[2 + d].wait_recv()
    out_top[...] = wide_sum(out_top[...], zf_top[0], zf_top[1])
    step_f_pair(5, zy_emb, zs_emb, EMB_ROWS, zc_emb, 1)
    for d in range(2):
        zc_tow[1 + d].wait_recv()
    out_tow[...] = wide_sum(blocks(zy_tow, TOW_ROWS, 0), zf_tow[0], zf_tow[1])
    step_g_pair(zy_emb, zs_emb, zb_emb, EMB_ROWS, zc_emb, 1)
    for d in range(2):
        zc_emb[1 + d].wait_recv()
    out_emb[...] = wide_sum(blocks(zy_emb, EMB_ROWS, 0), zf_emb[0], zf_emb[1])

    for q in range(PHASES):
        for d in range(2):
            zl_copy(q, d).wait_send()
            x_copy(q, d).wait_send()
            n_copy(q, d).wait_send()
        b_copy(q).wait_send()
    for p in range(PHASES + 2):
        for d in range(2):
            for h in range(NY // 2):
                y_copy(p, d, h).wait_send()
    for copy in zc_top + zc_tow + zc_emb:
        copy.wait_send()


def local(
    top_cot, top_pre, top_weight, tower_pre, tower_weight, pooled, feature_ids, bag_lengths, block_slot
):
    ids = jnp.transpose(feature_ids[0, :, 0], (1, 2, 0))
    lens = jnp.transpose(bag_lengths[0], (2, 1, 0))
    vmem, hbm = pl.BlockSpec(memory_space=pltpu.VMEM), pl.BlockSpec(memory_space=pltpu.HBM)
    dma = pltpu.SemaphoreType.DMA
    pieces = PHASES + 2
    outs = pl.pallas_call(
        kernel,
        out_shape=(
            jax.ShapeDtypeStruct((WOUT, LANES), F32),
            jax.ShapeDtypeStruct((TOW_ROWS, WOUT), F32),
            jax.ShapeDtypeStruct((EMB_ROWS, EMB), F32),
        ),
        in_specs=[hbm] * 9,
        out_specs=(vmem, vmem, vmem),
        scratch_shapes=[
            pltpu.VMEM((SHARD, TOPW), BF16),
            pltpu.VMEM((SHARD, TOPW), BF16),
            pltpu.VMEM((GROUP, WOUT), BF16),
            pltpu.VMEM((FEATS, BAG, GROUP), jnp.int32),
            pltpu.VMEM((FEATS, 1, GROUP), jnp.int32),
            pltpu.VMEM((1, NBLK), jnp.int32),
            pltpu.VMEM((PHASES, NZL, NX, NC, SHARD, WIDE), BF16),
            pltpu.VMEM((PHASES, WOUT, WIDE), BF16),
            pltpu.VMEM((SLAB, WOUT), BF16),
            pltpu.VMEM((GROUP, SLAB), BF16),
            pltpu.VMEM((SLAB, GROUP), BF16),
            pltpu.VMEM((WOUT, GROUP), BF16),
            pltpu.VMEM((GROUP, WOUT), F32),
            pltpu.VMEM((GROUP, WOUT), F32),
            pltpu.VMEM((GROUP, WOUT), BF16),
            pltpu.VMEM((FEATS, FROWS, GROUP), BF16),
            pltpu.VMEM((FEATS * FROWS, EMB), F32),
            pltpu.VMEM((NBLK * BLK, EMB), F32),
            pltpu.VMEM((PHASES, NY, WOUT, LANES), BF16),
            pltpu.VMEM((SLAB, WOUT), BF16),
            pltpu.VMEM((NBLK * BLK, EMB), BF16),
            pltpu.VMEM((PHASES, 2, NY // 2, WOUT, LANES), BF16),
            pltpu.VMEM((2, NY // 2, NZH * TOW_ROWS, WOUT), BF16),
            pltpu.VMEM((2, NY // 2, NZH * EMB_ROWS, EMB), BF16),
            pltpu.VMEM((3, WOUT, LANES), BF16),
            pltpu.VMEM((2, WOUT // 2, LANES), BF16),
            pltpu.VMEM((2, WOUT, LANES), BF16),
            pltpu.VMEM((NZH * TOW_ROWS, WOUT), F32),
            pltpu.VMEM((3, TOW_ROWS, WOUT), BF16),
            pltpu.VMEM((TOW_ROWS, WOUT), BF16),
            pltpu.VMEM((2, TOW_ROWS, WOUT), BF16),
            pltpu.VMEM((NZH * EMB_ROWS, EMB), F32),
            pltpu.VMEM((3, EMB_ROWS, EMB), BF16),
            pltpu.VMEM((EMB_ROWS, EMB), BF16),
            pltpu.VMEM((2, EMB_ROWS, EMB), BF16),
            dma((8,)),
            dma((PHASES,)),
            dma((PHASES, 2)),
            dma((PHASES, 2)),
            dma((PHASES, 2)),
            dma((PHASES, 2)),
            dma((PHASES, 2)),
            dma((PHASES, 2)),
            dma((PHASES,)),
            dma((PHASES,)),
            dma((pieces, 2, NY // 2)),
            dma((pieces, 2, NY // 2)),
            dma((10,)),
            dma((10,)),
        ],
        compiler_params=pltpu.CompilerParams(
            collective_id=0, has_side_effects=True, vmem_limit_bytes=64 * 1024 * 1024
        ),
    )(
        top_cot[0], top_pre[0], tower_pre[0], ids, lens, block_slot.reshape(1, NBLK), top_weight,
        tower_weight[0], pooled[0, :, 0, :],
    )
    return outs[0], outs[1][None], outs[2].reshape(1, NBLK // (NY * NZH), BLK, EMB)


def solution(mesh):
    placed = (
        P("local", "tower", None),
        P("local", "tower", None),
        P("tower", None),
        P("local", None, "tower"),
        P("tower", None, None),
        P("local", None, "tower", None),
        P("local", None, "tower", None, None),
        P("local", None, "tower", None),
        P(),
    )
    return jax.shard_map(
        local,
        mesh=mesh,
        in_specs=placed,
        out_specs=(P("tower", "local"), P("tower", "local", None), P("tower", "local", None, None)),
        check_vma=False,
    )
```

```python
import math

import jax
import jax.numpy as jnp
from jax import lax
from jax.experimental import pallas as pl
from jax.experimental.pallas import tpu as pltpu
from jax.sharding import PartitionSpec as P

MESH = pl.DeviceIdType.MESH
F32, BF16 = jnp.float32, jnp.bfloat16

NZL, NX, NC, NY, NZH = 3, 4, 2, 8, 4
TOPW, WOUT, FEATS, EMB, BAG, FROWS, BLK = 4096, 256, 12, 128, 4, 256, 32
GROUP, SLAB, NBLK = 384, 1536, 96
SHARD = GROUP // (NZL * NX * NC)
LANES = TOPW // (NY * NZH)
PARTS = NZH
OFF = (2, 1, 3, 0)
WIDE = PARTS * LANES
HALF_WIDE = WIDE // 2
AWAY = (4, 3, 5, 2, 6, 1, 7, 0)
GROUPS = ((0, 1), (1, 3), (3, 5), (5, 8))
TOW_ROWS = SLAB // (NY * NZH)
EMB_ROWS = NBLK * BLK // (NY * NZH)
FACTOR = 1.0 / math.sqrt(12288)


def gelu_value(values):
    return 0.5 * values * (1.0 + lax.erf(values / math.sqrt(2.0)))


def gelu_slope(values):
    return 0.5 * (1.0 + lax.erf(values / math.sqrt(2.0))) + values * jnp.exp(
        -0.5 * values * values
    ) / math.sqrt(2.0 * math.pi)


def wide_sum(*terms):
    total = terms[0].astype(F32)
    for term in terms[1:]:
        total = total + term.astype(F32)
    return total


def kernel(
    cot_hbm, pre_hbm, tower_pre_hbm, ids_hbm, lens_hbm, slot_hbm, weight_hbm, tower_weight_hbm,
    pooled_hbm, out_top, out_tow, out_emb,
    cot, pre, tower_pre, ids, lens, slot, rows, weight, tower_weight, pooled, pooled_t, comp_t, slope, part, delta_t, counts, dense, slotted,
    top, tow, emb, rb_top, rb_tow, rb_emb,
    zs_top, zb_top, zf_top, zy_tow, zs_tow, zb_tow, zf_tow, zy_emb, zs_emb, zb_emb, zf_emb,
    load_sem, weight_sem, zl_send, zl_recv, x_send, x_recv, n_send, n_recv, b_send, b_recv,
    y_send, y_recv, zh_send, zh_recv,
):
    t, l = lax.axis_index("tower"), lax.axis_index("local")
    core, x, zl = lax.rem(t, NC), lax.rem(lax.div(t, NC), NX), lax.div(t, NC * NX)
    y, zh = lax.div(l, NZH), lax.rem(l, NZH)

    def at_tower(zl_, x_, core_):
        return ((zl_ * NX + x_) * NC + core_, l)

    def at_local(y_, zh_):
        return (t, y_ * NZH + zh_)

    xp, xm = lax.rem(x + 1, NX), lax.rem(x + NX - 1, NX)
    xo = lax.rem(x + 2, NX)
    zl_next = [lax.rem(zl + d, NZL) for d in (1, 2)]
    zl_prev = [lax.rem(zl + NZL - d, NZL) for d in (1, 2)]
    y_next = [lax.rem(y + 1, NY), lax.rem(y + NY - 1, NY)]
    zh_next = [lax.rem(zh + 1, NZH), lax.rem(zh + NZH - 1, NZH)]
    dev_zl = [at_tower(zl_, x, core) for zl_ in zl_next]
    dev_x = [at_tower(zl, x_, core) for x_ in (xp, xm)]
    dev_sib = at_tower(zl, x, 1 - core)
    dev_y = [at_local(y_, zh) for y_ in y_next]
    dev_zh = [at_local(y, zh_) for zh_ in zh_next]

    barrier = pltpu.get_barrier_semaphore()
    peers = dev_zl + dev_x + [dev_sib] + dev_y + dev_zh

    def first_column(q, k):
        owner = lax.rem(y + k, NY) * NZH + lax.rem(zh + OFF[q], NZH)
        return pl.multiple_of(owner * LANES, LANES)

    def remote(src, dst, send, recv, device):
        return pltpu.make_async_remote_copy(
            src_ref=src, dst_ref=dst, send_sem=send, recv_sem=recv,
            device_id=device, device_id_type=MESH,
        )

    loads = [
        pltpu.make_async_copy(src, dst, load_sem.at[i])
        for i, (src, dst) in enumerate(
            [
                (cot_hbm, cot), (pre_hbm, pre), (tower_pre_hbm, tower_pre), (ids_hbm, ids),
                (lens_hbm, lens), (slot_hbm, slot), (pooled_hbm, pooled),
                (tower_weight_hbm, tower_weight),
            ]
        )
    ]
    load_cot, load_pre, load_tower_pre, load_ids, load_lens, load_slot, load_pool, load_tw = loads
    load_cot.start()
    load_pre.start()
    for peer in peers:
        pl.semaphore_signal(barrier, inc=1, device_id=peer, device_id_type=MESH)

    def load_rest():
        load_tower_pre.start()
        load_ids.start()
        load_lens.start()
        for g, (first, last) in enumerate(GROUPS):
            for j in range(first, last):
                for q in range(PARTS):
                    pltpu.make_async_copy(
                        weight_hbm.at[:, pl.ds(first_column(q, AWAY[j]), LANES)],
                        weight.at[j, :, pl.ds(q * LANES, LANES)],
                        weight_sem.at[g],
                    ).start()
        load_pool.start()
        load_tw.start()
        load_slot.start()

    def compute_delta(g):
        for j in range(*GROUPS[g]):
            for q in range(PARTS):
                cols = pl.ds(first_column(q, AWAY[j]), LANES)
                value = cot[:, cols].astype(F32) * gelu_slope(pre[:, cols].astype(F32))
                rows[j, zl, x, core, :, pl.ds(q * LANES, LANES)] = value.astype(BF16)

    def group(g):
        first, last = GROUPS[g]
        return rows.at[pl.ds(first, last - first)]

    def zl_copy(g, d):
        here = group(g).at[:, zl, x, core]
        return remote(here, here, zl_send.at[g, d], zl_recv.at[g, d], dev_zl[d])

    def zl_arrival(g, d):
        there = group(g).at[:, zl_prev[d], x, core]
        return remote(there, there, zl_send.at[g, d], zl_recv.at[g, d], dev_zl[1 - d])

    def x_copy(g, d):
        here = group(g).at[:, :, x, core]
        return remote(here, here, x_send.at[g, d], x_recv.at[g, d], dev_x[d])

    def x_arrival(g, d):
        there = group(g).at[:, :, (xm, xp)[d], core]
        return remote(there, there, x_send.at[g, d], x_recv.at[g, d], dev_x[1 - d])

    def n_copy(g, d):
        there = group(g).at[:, :, (xm, xp)[d], core, :, pl.ds(d * HALF_WIDE, HALF_WIDE)]
        return remote(there, there, n_send.at[g, d], n_recv.at[g, d], dev_x[d])

    def n_arrival(g, d):
        there = group(g).at[:, :, xo, core, :, pl.ds(d * HALF_WIDE, HALF_WIDE)]
        return remote(there, there, n_send.at[g, d], n_recv.at[g, d], dev_x[1 - d])

    def b_copy(g):
        here = group(g).at[:, :, :, core]
        return remote(here, here, b_send.at[g], b_recv.at[g], dev_sib)

    def b_arrival(g):
        there = group(g).at[:, :, :, 1 - core]
        return remote(there, there, b_send.at[g], b_recv.at[g], dev_sib)

    def step_z(g):
        for d in range(2):
            zl_copy(g, d).start()

    def step_x(g):
        for d in range(2):
            zl_arrival(g, d).wait_recv()
        for d in range(2):
            x_copy(g, d).start()

    def step_n(g, d):
        x_arrival(g, d).wait_recv()
        n_copy(g, d).start()

    def step_b(g):
        for d in range(2):
            n_arrival(g, d).wait_recv()
        b_copy(g).start()

    half_rows = [WOUT // 2] * PARTS + [NZH * TOW_ROWS // 2, NZH * EMB_ROWS // 2]

    def chunk(p, k):
        if p < PARTS:
            return top.at[p, k]
        y_ = lax.rem(y + k, NY)
        if p == PARTS:
            return tow.at[pl.ds(pl.multiple_of(y_ * (NZH * TOW_ROWS), 16), NZH * TOW_ROWS)]
        return emb.at[pl.ds(pl.multiple_of(y_ * (NZH * EMB_ROWS), 16), NZH * EMB_ROWS)]

    def landing(p, d, h):
        ref = rb_top.at[p, d, h] if p < PARTS else (rb_tow, rb_emb)[p - PARTS].at[d, h]
        return ref.at[pl.ds(0, half_rows[p])] if h == 0 else ref

    def half(p, d):
        return pl.ds(d * half_rows[p], half_rows[p])

    def y_copy(p, d, h):
        if h == 0:
            src = chunk(p, NY // 2).at[half(p, d)]
        else:
            src = chunk(p, NY // 2 - h if d == 0 else NY // 2 + h)
        return remote(src, landing(p, d, h), y_send.at[p, d, h], y_recv.at[p, d, h], dev_y[d])

    def step_s(p):
        for d in range(2):
            y_copy(p, d, 0).start()

    def step_h(p, h, d):
        y_copy(p, d, h - 1).wait_recv()
        own = chunk(p, NY // 2 - h if d == 0 else NY // 2 + h)
        if h == 1:
            own = own.at[half(p, d)]
        own[...] = wide_sum(own[...], landing(p, d, h - 1)[...]).astype(BF16)
        y_copy(p, d, h).start()

    def y_total(p):
        last = NY // 2 - 1
        for d in range(2):
            y_copy(p, d, last).wait_recv()
        return wide_sum(chunk(p, 0)[...], landing(p, 0, last)[...], landing(p, 1, last)[...])

    def zh_copy(i, src, dst, d):
        return remote(src, dst, zh_send.at[i], zh_recv.at[i], dev_zh[d])

    top_halves = [pl.ds(d * (WOUT // 2), WOUT // 2) for d in range(2)]
    zc_top = [zh_copy(d, zs_top.at[0, top_halves[d]], zb_top.at[d], d) for d in range(2)]
    zc_top += [zh_copy(2 + d, zs_top.at[1 + d], zf_top.at[d], d) for d in range(2)]
    zc_tow = [zh_copy(4, zs_tow.at[0], zb_tow, 0)]
    zc_tow += [zh_copy(5 + d, zs_tow.at[1 + d], zf_tow.at[d], d) for d in range(2)]
    zc_emb = [zh_copy(7, zs_emb.at[0], zb_emb, 1)]
    zc_emb += [zh_copy(8 + d, zs_emb.at[1 + d], zf_emb.at[d], d) for d in range(2)]

    def step_f_top(q):
        total = y_total(q)
        if q == 0:
            zs_top[0] = total.astype(BF16)
            for d in range(2):
                zc_top[d].start()
        elif q < 3:
            d = q - 1
            zc_top[d].wait_recv()
            zs_top[q] = total.astype(BF16)
            zs_top[q, top_halves[d]] = wide_sum(
                total[d * (WOUT // 2) : (d + 1) * (WOUT // 2)], zb_top[d]
            ).astype(BF16)
            zc_top[q + 1].start()
        else:
            out_top[...] = total

    def blocks(ref, size, offset):
        first = lax.rem(zh + offset, NZH) * size
        return ref[pl.ds(pl.multiple_of(first, 16), size), :]

    def step_f_pair(p, zy, zs, size, copies, via):
        zy[...] = y_total(p)
        zs[0] = blocks(zy, size, 2).astype(BF16)
        copies[0].start()
        zs[2 - via] = blocks(zy, size, (1, 3)[1 - via]).astype(BF16)
        copies[2 - via].start()

    def step_g_pair(zy, zs, zb, size, copies, via):
        copies[0].wait_recv()
        zs[1 + via] = wide_sum(blocks(zy, size, (1, 3)[via]), zb[...]).astype(BF16)
        copies[1 + via].start()

    def prepare_pre():
        load_tower_pre.wait()
        values = tower_pre[...].astype(F32)
        slope[...] = gelu_slope(values)
        comp_t[...] = gelu_value(values).T.astype(BF16)

    def prepare_counts(first, last):
        size = 64
        if first == 0:
            load_ids.wait()
            load_lens.wait()

        def feature(f, carry):
            length = lens[f]
            masked = [jnp.where(j < length, ids[f, j : j + 1, :], -1) for j in range(BAG)]
            for part_ in range(FROWS // size):
                table = lax.broadcasted_iota(jnp.int32, (size, GROUP), 0) + part_ * size
                hits = [jnp.where(m == table, 1.0, 0.0) for m in masked]
                count = (hits[0] + hits[1]) + (hits[2] + hits[3])
                counts[f, pl.ds(part_ * size, size), :] = count.astype(BF16)
            return carry

        lax.fori_loop(first, last, feature, 0)

    def prepare_pooled(first, last):
        if first == 0:
            load_pool.wait()
        for c in range(first, last):
            block = pooled[:, c * EMB : (c + 1) * EMB].astype(F32)
            pooled_t[c * EMB : (c + 1) * EMB, :] = block.T.astype(BF16)

    def compute_top(g):
        b_arrival(g).wait_recv()
        for j in range(*GROUPS[g]):
            deltas = rows[j].reshape(GROUP, WIDE)
            term = jnp.dot(comp_t[...], deltas, preferred_element_type=F32) * FACTOR
            for q in range(PARTS):
                top[q, AWAY[j]] = term[:, q * LANES : (q + 1) * LANES].astype(BF16)

    def compute_part(g):
        first, last = GROUPS[g]
        loaded = weight.at[pl.ds(first, last - first)]
        pltpu.make_async_copy(loaded, loaded, weight_sem.at[g]).wait()
        for j in range(first, last):
            product = lax.dot_general(
                rows[j].reshape(GROUP, WIDE), weight[j],
                (((1,), (1,)), ((), ())), preferred_element_type=F32,
            )
            part[...] = product if j == 0 else part[...] + product

    def compute_tow():
        feature_grad = part[...].astype(BF16).astype(F32)
        delta_t[...] = (feature_grad * slope[...]).astype(BF16)
        for c in range(0, SLAB, 256):
            term = jnp.dot(pooled_t[c : c + 256, :], delta_t[...], preferred_element_type=F32)
            tow[c : c + 256, :] = (term * FACTOR).astype(BF16)

    def compute_emb():
        load_tw.wait()
        for f in range(FEATS):
            grad = lax.dot_general(
                delta_t[...], tower_weight[f * EMB : (f + 1) * EMB, :],
                (((1,), (1,)), ((), ())), preferred_element_type=F32,
            ).astype(BF16)
            dense[f * FROWS : (f + 1) * FROWS, :] = jnp.dot(
                counts[f], grad, preferred_element_type=F32
            )
        load_slot.wait()
        numbers = lax.broadcasted_iota(jnp.int32, (NBLK, NBLK), 0)
        moves = jnp.where(slot[...] == numbers, 1.0, 0.0).astype(BF16)
        for i in range(0, BLK, 2):
            taken = [dense[pl.ds(i + j, NBLK, stride=BLK), :].astype(BF16) for j in range(2)]
            moved = jnp.dot(moves, jnp.concatenate(taken, 1), preferred_element_type=F32)
            for j in range(2):
                slotted[pl.ds(i + j, NBLK, stride=BLK), :] = moved[:, j * EMB : (j + 1) * EMB]
        emb[...] = slotted[...].astype(BF16)

    load_cot.wait()
    load_pre.wait()
    compute_delta(0)
    pl.semaphore_wait(barrier, len(peers))
    step_z(0)
    compute_delta(1)
    step_z(1)
    compute_delta(2)
    step_z(2)
    compute_delta(3)
    step_z(3)
    load_rest()
    prepare_pre()
    step_x(0)
    prepare_counts(0, 4)
    step_x(1)
    step_n(0, 0)
    step_n(0, 1)
    prepare_counts(4, 8)
    step_x(2)
    step_b(0)
    step_n(1, 0)
    step_n(1, 1)
    step_x(3)
    prepare_counts(8, 12)
    compute_top(0)
    for p in range(PARTS):
        step_s(p)
    step_b(1)
    step_n(2, 0)
    step_n(2, 1)
    prepare_pooled(0, 6)
    compute_top(1)
    step_h(0, 1, 0)
    step_h(0, 1, 1)
    step_h(1, 1, 0)
    step_h(1, 1, 1)
    step_h(2, 1, 0)
    step_h(2, 1, 1)
    step_h(3, 1, 0)
    step_h(3, 1, 1)
    step_b(2)
    step_n(3, 0)
    step_n(3, 1)
    compute_part(0)
    compute_part(1)
    compute_top(2)
    prepare_pooled(6, 12)
    step_h(0, 2, 0)
    step_h(0, 2, 1)
    step_h(1, 2, 0)
    step_h(1, 2, 1)
    step_b(3)
    compute_part(2)
    step_h(2, 2, 0)
    step_h(2, 2, 1)
    step_h(3, 2, 0)
    step_h(3, 2, 1)
    compute_top(3)
    compute_part(3)
    compute_tow()
    step_s(4)
    step_h(0, 3, 0)
    step_h(0, 3, 1)
    step_h(1, 3, 0)
    step_h(1, 3, 1)
    compute_emb()
    step_s(5)
    step_h(4, 1, 0)
    step_h(4, 1, 1)
    step_h(2, 3, 0)
    step_h(2, 3, 1)
    step_f_top(0)
    step_h(5, 1, 0)
    step_h(5, 1, 1)
    step_h(4, 2, 0)
    step_h(4, 2, 1)
    step_f_top(1)
    step_h(5, 2, 0)
    step_h(5, 2, 1)
    step_f_top(2)
    step_h(4, 3, 0)
    step_h(4, 3, 1)
    step_h(5, 3, 0)
    step_h(5, 3, 1)
    step_h(3, 3, 0)
    step_h(3, 3, 1)
    step_f_pair(4, zy_tow, zs_tow, TOW_ROWS, zc_tow, 0)
    step_f_pair(5, zy_emb, zs_emb, EMB_ROWS, zc_emb, 1)
    step_g_pair(zy_tow, zs_tow, zb_tow, TOW_ROWS, zc_tow, 0)
    step_g_pair(zy_emb, zs_emb, zb_emb, EMB_ROWS, zc_emb, 1)
    for d in range(2):
        zc_tow[1 + d].wait_recv()
    out_tow[...] = wide_sum(blocks(zy_tow, TOW_ROWS, 0), zf_tow[0], zf_tow[1])
    step_f_top(3)
    for d in range(2):
        zc_top[2 + d].wait_recv()
    out_top[...] = wide_sum(out_top[...], zf_top[0], zf_top[1])
    for d in range(2):
        zc_emb[1 + d].wait_recv()
    out_emb[...] = wide_sum(blocks(zy_emb, EMB_ROWS, 0), zf_emb[0], zf_emb[1])

    for g in range(len(GROUPS)):
        for d in range(2):
            zl_copy(g, d).wait_send()
            x_copy(g, d).wait_send()
            n_copy(g, d).wait_send()
        b_copy(g).wait_send()
    for p in range(PARTS + 2):
        for d in range(2):
            for h in range(NY // 2):
                y_copy(p, d, h).wait_send()
    for copy in zc_top + zc_tow + zc_emb:
        copy.wait_send()


def place(*refs):
    sources, results, held, sems = refs[:3], refs[3:6], refs[6:9], refs[9]
    first = [pltpu.make_async_copy(*two, sems.at[0, i]) for i, two in enumerate(zip(sources, held))]
    second = [pltpu.make_async_copy(*two, sems.at[1, i]) for i, two in enumerate(zip(held, results))]
    for copy in first:
        copy.start()
    for one, two in zip(first, second):
        one.wait()
        two.start()
    for copy in second:
        copy.wait()


def local(
    top_cot, top_pre, top_weight, tower_pre, tower_weight, pooled, feature_ids, bag_lengths, block_slot
):
    ids = jnp.transpose(feature_ids[0, :, 0], (1, 2, 0))
    lens = jnp.transpose(bag_lengths[0], (2, 1, 0))
    vmem, hbm = pl.BlockSpec(memory_space=pltpu.VMEM), pl.BlockSpec(memory_space=pltpu.HBM)
    dma = pltpu.SemaphoreType.DMA
    pieces = PARTS + 2
    shapes = (
        jax.ShapeDtypeStruct((WOUT, LANES), F32),
        jax.ShapeDtypeStruct((TOW_ROWS, WOUT), F32),
        jax.ShapeDtypeStruct((EMB_ROWS, EMB), F32),
    )
    outs = pl.pallas_call(
        kernel,
        out_shape=shapes,
        in_specs=[hbm] * 9,
        out_specs=(vmem, vmem, vmem),
        scratch_shapes=[
            pltpu.VMEM((SHARD, TOPW), BF16),
            pltpu.VMEM((SHARD, TOPW), BF16),
            pltpu.VMEM((GROUP, WOUT), BF16),
            pltpu.VMEM((FEATS, BAG, GROUP), jnp.int32),
            pltpu.VMEM((FEATS, 1, GROUP), jnp.int32),
            pltpu.VMEM((1, NBLK), jnp.int32),
            pltpu.VMEM((NY, NZL, NX, NC, SHARD, WIDE), BF16),
            pltpu.VMEM((NY, WOUT, WIDE), BF16),
            pltpu.VMEM((SLAB, WOUT), BF16),
            pltpu.VMEM((GROUP, SLAB), BF16),
            pltpu.VMEM((SLAB, GROUP), BF16),
            pltpu.VMEM((WOUT, GROUP), BF16),
            pltpu.VMEM((GROUP, WOUT), F32),
            pltpu.VMEM((GROUP, WOUT), F32),
            pltpu.VMEM((GROUP, WOUT), BF16),
            pltpu.VMEM((FEATS, FROWS, GROUP), BF16),
            pltpu.VMEM((FEATS * FROWS, EMB), F32),
            pltpu.VMEM((NBLK * BLK, EMB), F32),
            pltpu.VMEM((PARTS, NY, WOUT, LANES), BF16),
            pltpu.VMEM((SLAB, WOUT), BF16),
            pltpu.VMEM((NBLK * BLK, EMB), BF16),
            pltpu.VMEM((PARTS, 2, NY // 2, WOUT, LANES), BF16),
            pltpu.VMEM((2, NY // 2, NZH * TOW_ROWS, WOUT), BF16),
            pltpu.VMEM((2, NY // 2, NZH * EMB_ROWS, EMB), BF16),
            pltpu.VMEM((3, WOUT, LANES), BF16),
            pltpu.VMEM((2, WOUT // 2, LANES), BF16),
            pltpu.VMEM((2, WOUT, LANES), BF16),
            pltpu.VMEM((NZH * TOW_ROWS, WOUT), F32),
            pltpu.VMEM((3, TOW_ROWS, WOUT), BF16),
            pltpu.VMEM((TOW_ROWS, WOUT), BF16),
            pltpu.VMEM((2, TOW_ROWS, WOUT), BF16),
            pltpu.VMEM((NZH * EMB_ROWS, EMB), F32),
            pltpu.VMEM((3, EMB_ROWS, EMB), BF16),
            pltpu.VMEM((EMB_ROWS, EMB), BF16),
            pltpu.VMEM((2, EMB_ROWS, EMB), BF16),
            dma((8,)),
            dma((len(GROUPS),)),
            dma((len(GROUPS), 2)),
            dma((len(GROUPS), 2)),
            dma((len(GROUPS), 2)),
            dma((len(GROUPS), 2)),
            dma((len(GROUPS), 2)),
            dma((len(GROUPS), 2)),
            dma((len(GROUPS),)),
            dma((len(GROUPS),)),
            dma((pieces, 2, NY // 2)),
            dma((pieces, 2, NY // 2)),
            dma((10,)),
            dma((10,)),
        ],
        compiler_params=pltpu.CompilerParams(
            collective_id=0, has_side_effects=True, vmem_limit_bytes=64 * 1024 * 1024
        ),
    )(
        top_cot[0], top_pre[0], tower_pre[0], ids, lens, block_slot.reshape(1, NBLK), top_weight,
        tower_weight[0], pooled[0, :, 0, :],
    )
    outs = pl.pallas_call(
        place,
        out_shape=shapes,
        in_specs=[hbm] * 3,
        out_specs=(hbm, hbm, hbm),
        scratch_shapes=[pltpu.VMEM(s.shape, F32) for s in shapes] + [dma((2, 3))],
        compiler_params=pltpu.CompilerParams(vmem_limit_bytes=64 * 1024 * 1024),
    )(*outs)
    return outs[0], outs[1][None], outs[2].reshape(1, NBLK // (NY * NZH), BLK, EMB)


def solution(mesh):
    placed = (
        P("local", "tower", None),
        P("local", "tower", None),
        P("tower", None),
        P("local", None, "tower"),
        P("tower", None, None),
        P("local", None, "tower", None),
        P("local", None, "tower", None, None),
        P("local", None, "tower", None),
        P(),
    )
    return jax.shard_map(
        local,
        mesh=mesh,
        in_specs=placed,
        out_specs=(P("tower", "local"), P("tower", "local", None), P("tower", "local", None, None)),
        check_vma=False,
    )
```

```python
import math

import jax
import jax.numpy as jnp
from jax import lax
from jax.experimental import pallas as pl
from jax.experimental.pallas import tpu as pltpu
from jax.sharding import PartitionSpec as P

MESH = pl.DeviceIdType.MESH
F32, BF16 = jnp.float32, jnp.bfloat16

NZL, NX, NC, NY, NZH = 3, 4, 2, 8, 4
TOPW, WOUT, FEATS, EMB, BAG, FROWS, BLK = 4096, 256, 12, 128, 4, 256, 32
GROUP, SLAB, NBLK = 384, 1536, 96
SHARD = GROUP // (NZL * NX * NC)
LANES = TOPW // (NY * NZH)
PARTS = NZH
OFF = (2, 1, 3, 0)
WIDE = PARTS * LANES
AWAY = (4, 3, 5, 2, 6, 1, 7, 0)
SPANS = ((0, 1), (1, 3), (3, 5), (5, 8))
GROUPS = ((0, 0, 4), (1, 0, 4), (2, 0, 4), (3, 0, 4))
TOW_ROWS = SLAB // (NY * NZH)
EMB_ROWS = NBLK * BLK // (NY * NZH)
FACTOR = 1.0 / math.sqrt(12288)


def gelu_value(values):
    return 0.5 * values * (1.0 + lax.erf(values / math.sqrt(2.0)))


def gelu_slope(values):
    return 0.5 * (1.0 + lax.erf(values / math.sqrt(2.0))) + values * jnp.exp(
        -0.5 * values * values
    ) / math.sqrt(2.0 * math.pi)


def wide_sum(*terms):
    total = terms[0].astype(F32)
    for term in terms[1:]:
        total = total + term.astype(F32)
    return total


def kernel(
    cot_hbm, pre_hbm, tower_pre_hbm, ids_hbm, lens_hbm, slot_hbm, weight_hbm, tower_weight_hbm,
    pooled_hbm, top_hbm, tow_hbm, emb_hbm,
    out_top, out_tow, out_emb,
    cot, pre, tower_pre, ids, lens, slot, rows, weight, tower_weight, pooled, pooled_t, comp_t, slope, part, delta_t, counts, dense, slotted,
    top, tow, emb, rb_top, rb_tow, rb_emb,
    zs_top, zb_top, zf_top, zy_tow, zs_tow, zf_tow, zy_emb, zs_emb, zf_emb,
    load_sem, weight_sem, zl_send, zl_recv, x_send, x_recv, b_send, b_recv,
    y_send, y_recv, zh_send, zh_recv,
):
    t, l = lax.axis_index("tower"), lax.axis_index("local")
    core, x, zl = lax.rem(t, NC), lax.rem(lax.div(t, NC), NX), lax.div(t, NC * NX)
    y, zh = lax.div(l, NZH), lax.rem(l, NZH)

    def at_tower(zl_, x_, core_):
        return ((zl_ * NX + x_) * NC + core_, l)

    def at_local(y_, zh_):
        return (t, y_ * NZH + zh_)

    xp, xm = lax.rem(x + 1, NX), lax.rem(x + NX - 1, NX)
    xo = lax.rem(x + 2, NX)
    zl_next = [lax.rem(zl + d, NZL) for d in (1, 2)]
    zl_prev = [lax.rem(zl + NZL - d, NZL) for d in (1, 2)]
    y_next = [lax.rem(y + 1, NY), lax.rem(y + NY - 1, NY)]
    zh_next = [lax.rem(zh + 1, NZH), lax.rem(zh + NZH - 1, NZH)]
    dev_zl = [at_tower(zl_, x, core) for zl_ in zl_next]
    x_next, x_prev = (xp, xm, xo), (xm, xp, xo)
    dev_x = [at_tower(zl, x_, core) for x_ in x_next]
    dev_x_prev = [at_tower(zl, x_, core) for x_ in x_prev]
    dev_sib = at_tower(zl, x, 1 - core)
    dev_y = [at_local(y_, zh) for y_ in y_next]
    dev_zh = [at_local(y, zh_) for zh_ in zh_next + [lax.rem(zh + 2, NZH)]]

    barrier = pltpu.get_barrier_semaphore()
    peers = dev_zl + dev_x + [dev_sib] + dev_y + dev_zh

    def first_column(q, k):
        owner = lax.rem(y + k, NY) * NZH + lax.rem(zh + OFF[q], NZH)
        return pl.multiple_of(owner * LANES, LANES)

    def remote(src, dst, send, recv, device):
        return pltpu.make_async_remote_copy(
            src_ref=src, dst_ref=dst, send_sem=send, recv_sem=recv,
            device_id=device, device_id_type=MESH,
        )

    loads = [
        pltpu.make_async_copy(src, dst, load_sem.at[i])
        for i, (src, dst) in enumerate(
            [
                (cot_hbm, cot), (pre_hbm, pre), (tower_pre_hbm, tower_pre), (ids_hbm, ids),
                (lens_hbm, lens), (slot_hbm, slot), (pooled_hbm, pooled),
                (tower_weight_hbm, tower_weight),
            ]
        )
    ]
    put_top, put_tow, put_emb = [
        pltpu.make_async_copy(src, dst, load_sem.at[8 + i])
        for i, (src, dst) in enumerate(
            [(out_top, top_hbm), (out_tow, tow_hbm), (out_emb, emb_hbm)]
        )
    ]
    load_cot, load_pre, load_tower_pre, load_ids, load_lens, load_slot, load_pool, load_tw = loads
    load_cot.start()
    load_pre.start()
    for peer in peers:
        pl.semaphore_signal(barrier, inc=1, device_id=peer, device_id_type=MESH)

    def load_rest():
        load_tower_pre.start()
        load_ids.start()
        load_lens.start()
        for g, (first, last) in enumerate(SPANS):
            for j in range(first, last):
                for q in range(PARTS):
                    pltpu.make_async_copy(
                        weight_hbm.at[:, pl.ds(first_column(q, AWAY[j]), LANES)],
                        weight.at[j, :, pl.ds(q * LANES, LANES)],
                        weight_sem.at[g],
                    ).start()
        load_pool.start()
        load_tw.start()
        load_slot.start()

    def compute_delta(g):
        span, low, high = GROUPS[g]
        for j in range(*SPANS[span]):
            for q in range(low, high):
                cols = pl.ds(first_column(q, AWAY[j]), LANES)
                value = cot[:, cols].astype(F32) * gelu_slope(pre[:, cols].astype(F32))
                rows[j, zl, x, core, :, pl.ds(q * LANES, LANES)] = value.astype(BF16)

    every = slice(None)

    def group(g, zl_, x_, core_, piece=0, pieces=1):
        span, low, high = GROUPS[g]
        first, last = SPANS[span]
        wide = (high - low) * LANES // pieces
        cols = pl.ds(low * LANES + piece * wide, wide)
        return rows.at[pl.ds(first, last - first), zl_, x_, core_, :, cols]

    def zl_copy(g, d):
        here = group(g, zl, x, core)
        return remote(here, here, zl_send.at[g, d], zl_recv.at[g, d], dev_zl[d])

    def zl_arrival(g, d):
        there = group(g, zl_prev[d], x, core)
        return remote(there, there, zl_send.at[g, d], zl_recv.at[g, d], dev_zl[1 - d])

    def x_copy(g, d):
        here = group(g, every, x, core)
        return remote(here, here, x_send.at[g, d], x_recv.at[g, d], dev_x[d])

    def x_arrival(g, d):
        there = group(g, every, x_prev[d], core)
        return remote(there, there, x_send.at[g, d], x_recv.at[g, d], dev_x_prev[d])

    def b_copy(g):
        here = group(g, every, every, core)
        return remote(here, here, b_send.at[g], b_recv.at[g], dev_sib)

    def b_arrival(g):
        there = group(g, every, every, 1 - core)
        return remote(there, there, b_send.at[g], b_recv.at[g], dev_sib)

    def step_z(g):
        for d in range(2):
            zl_copy(g, d).start()

    def step_x(g):
        for d in range(2):
            zl_arrival(g, d).wait_recv()
        for d in range(3):
            x_copy(g, d).start()

    def step_b(g):
        for d in range(3):
            x_arrival(g, d).wait_recv()
        b_copy(g).start()

    half_rows = [WOUT // 2] * PARTS + [NZH * TOW_ROWS // 2, NZH * EMB_ROWS // 2]

    def chunk(p, k):
        if p < PARTS:
            return top.at[p, k]
        y_ = lax.rem(y + k, NY)
        if p == PARTS:
            return tow.at[pl.ds(pl.multiple_of(y_ * (NZH * TOW_ROWS), 16), NZH * TOW_ROWS)]
        return emb.at[pl.ds(pl.multiple_of(y_ * (NZH * EMB_ROWS), 16), NZH * EMB_ROWS)]

    def landing(p, d, h):
        ref = rb_top.at[p, d, h] if p < PARTS else (rb_tow, rb_emb)[p - PARTS].at[d, h]
        return ref.at[pl.ds(0, half_rows[p])] if h == 0 else ref

    def half(p, d):
        return pl.ds(d * half_rows[p], half_rows[p])

    def y_copy(p, d, h):
        if h == 0:
            src = chunk(p, NY // 2).at[half(p, d)]
        else:
            src = chunk(p, NY // 2 - h if d == 0 else NY // 2 + h)
        return remote(src, landing(p, d, h), y_send.at[p, d, h], y_recv.at[p, d, h], dev_y[d])

    def step_s(p):
        for d in range(2):
            y_copy(p, d, 0).start()

    def step_h(p, h, d):
        y_copy(p, d, h - 1).wait_recv()
        own = chunk(p, NY // 2 - h if d == 0 else NY // 2 + h)
        if h == 1:
            own = own.at[half(p, d)]
        own[...] = wide_sum(own[...], landing(p, d, h - 1)[...]).astype(BF16)
        y_copy(p, d, h).start()

    def y_total(p):
        last = NY // 2 - 1
        for d in range(2):
            y_copy(p, d, last).wait_recv()
        return wide_sum(chunk(p, 0)[...], landing(p, 0, last)[...], landing(p, 1, last)[...])

    def zh_copy(i, src, dst, d):
        return remote(src, dst, zh_send.at[i], zh_recv.at[i], dev_zh[d])

    top_halves = [pl.ds(d * (WOUT // 2), WOUT // 2) for d in range(2)]
    zc_top = [zh_copy(d, zs_top.at[0, top_halves[d]], zb_top.at[d], d) for d in range(2)]
    zc_top += [zh_copy(2 + d, zs_top.at[1 + d], zf_top.at[d], d) for d in range(2)]
    zc_tow = [zh_copy(4 + d, zs_tow.at[d], zf_tow.at[d], d) for d in range(3)]
    zc_emb = [zh_copy(7 + d, zs_emb.at[d], zf_emb.at[d], d) for d in range(3)]

    def step_f_top(q):
        total = y_total(q)
        if q == 0:
            zs_top[0] = total.astype(BF16)
            for d in range(2):
                zc_top[d].start()
        elif q < 3:
            d = q - 1
            zc_top[d].wait_recv()
            zs_top[q] = total.astype(BF16)
            zs_top[q, top_halves[d]] = wide_sum(
                total[d * (WOUT // 2) : (d + 1) * (WOUT // 2)], zb_top[d]
            ).astype(BF16)
            zc_top[q + 1].start()
        else:
            out_top[...] = total

    def blocks(ref, size, offset):
        first = lax.rem(zh + offset, NZH) * size
        return ref[pl.ds(pl.multiple_of(first, 16), size), :]

    def step_f_pair(p, zy, zs, size, copies):
        zy[...] = y_total(p)
        for d in (2, 0, 1):
            zs[d] = blocks(zy, size, (1, 3, 2)[d]).astype(BF16)
            copies[d].start()

    def finish_pair(out, zy, zf, size, copies):
        for d in range(3):
            copies[d].wait_recv()
        out[...] = wide_sum(blocks(zy, size, 0), zf[0], zf[1], zf[2])

    def prepare_pre():
        load_tower_pre.wait()
        values = tower_pre[...].astype(F32)
        slope[...] = gelu_slope(values)
        comp_t[...] = gelu_value(values).T.astype(BF16)

    def prepare_counts(first, last):
        size = 64
        if first == 0:
            load_ids.wait()
            load_lens.wait()

        def feature(f, carry):
            length = lens[f]
            masked = [jnp.where(j < length, ids[f, j : j + 1, :], -1) for j in range(BAG)]
            for part_ in range(FROWS // size):
                table = lax.broadcasted_iota(jnp.int32, (size, GROUP), 0) + part_ * size
                hits = [jnp.where(m == table, 1.0, 0.0) for m in masked]
                count = (hits[0] + hits[1]) + (hits[2] + hits[3])
                counts[f, pl.ds(part_ * size, size), :] = count.astype(BF16)
            return carry

        lax.fori_loop(first, last, feature, 0)

    def prepare_pooled(first, last):
        if first == 0:
            load_pool.wait()
        for c in range(first, last):
            block = pooled[:, c * EMB : (c + 1) * EMB].astype(F32)
            pooled_t[c * EMB : (c + 1) * EMB, :] = block.T.astype(BF16)

    def compute_top(g):
        span, low, high = GROUPS[g]
        for j in range(*SPANS[span]):
            deltas = rows[j, :, :, :, :, low * LANES : high * LANES].reshape(GROUP, (high - low) * LANES)
            term = (jnp.dot(comp_t[...], deltas, preferred_element_type=F32) * FACTOR).astype(BF16)
            for q in range(low, high):
                value = term[:, (q - low) * LANES : (q - low + 1) * LANES]
                top[q, AWAY[j]] = value

    def compute_part(i):
        first, last = SPANS[i]
        loaded = weight.at[pl.ds(first, last - first)]
        pltpu.make_async_copy(loaded, loaded, weight_sem.at[i]).wait()
        for j in range(first, last):
            product = lax.dot_general(
                rows[j].reshape(GROUP, WIDE), weight[j],
                (((1,), (1,)), ((), ())), preferred_element_type=F32,
            )
            part[...] = product if j == 0 else part[...] + product

    def compute_tow():
        feature_grad = part[...].astype(BF16).astype(F32)
        delta_t[...] = (feature_grad * slope[...]).astype(BF16)
        for k in AWAY:
            first = lax.rem(y + k, NY) * (NZH * TOW_ROWS)
            here = pl.ds(pl.multiple_of(first, 16), NZH * TOW_ROWS)
            term = jnp.dot(pooled_t[here, :], delta_t[...], preferred_element_type=F32)
            tow[here, :] = (term * FACTOR).astype(BF16)
            if k == NY // 2:
                step_s(PARTS)

    def compute_emb():
        load_tw.wait()
        for f in range(FEATS):
            grad = lax.dot_general(
                delta_t[...], tower_weight[f * EMB : (f + 1) * EMB, :],
                (((1,), (1,)), ((), ())), preferred_element_type=F32,
            ).astype(BF16)
            dense[f * FROWS : (f + 1) * FROWS, :] = jnp.dot(
                counts[f], grad, preferred_element_type=F32
            )
        load_slot.wait()
        numbers = lax.broadcasted_iota(jnp.int32, (NBLK, NBLK), 0)
        moves = jnp.where(slot[...] == numbers, 1.0, 0.0).astype(BF16)
        for i in range(0, BLK, 2):
            taken = [dense[pl.ds(i + j, NBLK, stride=BLK), :].astype(BF16) for j in range(2)]
            moved = jnp.dot(moves, jnp.concatenate(taken, 1), preferred_element_type=F32)
            for j in range(2):
                slotted[pl.ds(i + j, NBLK, stride=BLK), :] = moved[:, j * EMB : (j + 1) * EMB]
        for k in AWAY:
            first = lax.rem(y + k, NY) * (NZH * EMB_ROWS)
            here = pl.ds(pl.multiple_of(first, 16), NZH * EMB_ROWS)
            emb[here, :] = slotted[here, :].astype(BF16)
            if k == NY // 2:
                step_s(PARTS + 1)

    load_cot.wait()
    load_pre.wait()
    compute_delta(0)
    pl.semaphore_wait(barrier, len(peers))
    step_z(0)
    compute_delta(1)
    step_z(1)
    compute_delta(2)
    step_z(2)
    compute_delta(3)
    step_z(3)
    load_rest()
    prepare_pre()
    step_x(0)
    step_x(1)
    prepare_counts(0, 4)
    step_x(2)
    step_b(0)
    step_x(3)
    prepare_counts(4, 8)
    b_arrival(0).wait_recv()
    compute_top(0)
    for p in range(PARTS):
        step_s(p)
    step_b(1)
    prepare_counts(8, 12)
    prepare_pooled(0, 6)
    b_arrival(1).wait_recv()
    compute_top(1)
    step_h(0, 1, 0)
    step_h(0, 1, 1)
    step_h(1, 1, 0)
    step_h(1, 1, 1)
    step_h(2, 1, 0)
    step_h(2, 1, 1)
    step_h(3, 1, 0)
    step_h(3, 1, 1)
    step_b(2)
    compute_part(0)
    compute_part(1)
    prepare_pooled(6, 12)
    b_arrival(2).wait_recv()
    compute_top(2)
    step_b(3)
    step_h(0, 2, 0)
    step_h(0, 2, 1)
    step_h(1, 2, 0)
    step_h(1, 2, 1)
    compute_part(2)
    step_h(2, 2, 0)
    step_h(2, 2, 1)
    step_h(3, 2, 0)
    step_h(3, 2, 1)
    b_arrival(3).wait_recv()
    compute_part(3)
    compute_tow()
    compute_top(3)
    step_h(0, 3, 0)
    step_h(0, 3, 1)
    step_h(1, 3, 0)
    step_h(1, 3, 1)
    compute_emb()
    step_h(4, 1, 0)
    step_h(4, 1, 1)
    step_h(2, 3, 0)
    step_h(2, 3, 1)
    step_f_top(0)
    step_h(5, 1, 0)
    step_h(5, 1, 1)
    step_h(4, 2, 0)
    step_h(4, 2, 1)
    step_f_top(1)
    step_h(5, 2, 0)
    step_h(5, 2, 1)
    step_f_top(2)
    step_h(4, 3, 0)
    step_h(4, 3, 1)
    step_h(5, 3, 0)
    step_h(5, 3, 1)
    step_h(3, 3, 0)
    step_h(3, 3, 1)
    step_f_pair(PARTS, zy_tow, zs_tow, TOW_ROWS, zc_tow)
    step_f_pair(PARTS + 1, zy_emb, zs_emb, EMB_ROWS, zc_emb)
    step_f_top(3)
    for d in range(2):
        zc_top[2 + d].wait_recv()
    out_top[...] = wide_sum(out_top[...], zf_top[0], zf_top[1])
    put_top.start()
    finish_pair(out_tow, zy_tow, zf_tow, TOW_ROWS, zc_tow)
    put_tow.start()
    finish_pair(out_emb, zy_emb, zf_emb, EMB_ROWS, zc_emb)
    put_emb.start()

    put_top.wait()
    put_tow.wait()
    put_emb.wait()
    for g in range(len(GROUPS)):
        for d in range(2):
            zl_copy(g, d).wait_send()
        for d in range(3):
            x_copy(g, d).wait_send()
        b_copy(g).wait_send()
    for p in range(PARTS + 2):
        for d in range(2):
            for h in range(NY // 2):
                y_copy(p, d, h).wait_send()
    for copy in zc_top + zc_tow + zc_emb:
        copy.wait_send()


def place(*refs):
    sources, results, held, sems = refs[:3], refs[3:6], refs[6:9], refs[9]
    first = [pltpu.make_async_copy(*two, sems.at[0, i]) for i, two in enumerate(zip(sources, held))]
    second = [pltpu.make_async_copy(*two, sems.at[1, i]) for i, two in enumerate(zip(held, results))]
    for copy in first:
        copy.start()
    for one, two in zip(first, second):
        one.wait()
        two.start()
    for copy in second:
        copy.wait()


def local(
    top_cot, top_pre, top_weight, tower_pre, tower_weight, pooled, feature_ids, bag_lengths, block_slot
):
    ids = jnp.transpose(feature_ids[0, :, 0], (1, 2, 0))
    lens = jnp.transpose(bag_lengths[0], (2, 1, 0))
    hbm = pl.BlockSpec(memory_space=pltpu.HBM)
    dma = pltpu.SemaphoreType.DMA
    pieces = PARTS + 2
    shapes = (
        jax.ShapeDtypeStruct((WOUT, LANES), F32),
        jax.ShapeDtypeStruct((TOW_ROWS, WOUT), F32),
        jax.ShapeDtypeStruct((EMB_ROWS, EMB), F32),
    )
    outs = pl.pallas_call(
        kernel,
        out_shape=shapes,
        in_specs=[hbm] * 9,
        out_specs=(hbm, hbm, hbm),
        scratch_shapes=[pltpu.VMEM(s.shape, F32) for s in shapes]
        + [
            pltpu.VMEM((SHARD, TOPW), BF16),
            pltpu.VMEM((SHARD, TOPW), BF16),
            pltpu.VMEM((GROUP, WOUT), BF16),
            pltpu.VMEM((FEATS, BAG, GROUP), jnp.int32),
            pltpu.VMEM((FEATS, 1, GROUP), jnp.int32),
            pltpu.VMEM((1, NBLK), jnp.int32),
            pltpu.VMEM((NY, NZL, NX, NC, SHARD, WIDE), BF16),
            pltpu.VMEM((NY, WOUT, WIDE), BF16),
            pltpu.VMEM((SLAB, WOUT), BF16),
            pltpu.VMEM((GROUP, SLAB), BF16),
            pltpu.VMEM((SLAB, GROUP), BF16),
            pltpu.VMEM((WOUT, GROUP), BF16),
            pltpu.VMEM((GROUP, WOUT), F32),
            pltpu.VMEM((GROUP, WOUT), F32),
            pltpu.VMEM((GROUP, WOUT), BF16),
            pltpu.VMEM((FEATS, FROWS, GROUP), BF16),
            pltpu.VMEM((FEATS * FROWS, EMB), F32),
            pltpu.VMEM((NBLK * BLK, EMB), F32),
            pltpu.VMEM((PARTS, NY, WOUT, LANES), BF16),
            pltpu.VMEM((SLAB, WOUT), BF16),
            pltpu.VMEM((NBLK * BLK, EMB), BF16),
            pltpu.VMEM((PARTS, 2, NY // 2, WOUT, LANES), BF16),
            pltpu.VMEM((2, NY // 2, NZH * TOW_ROWS, WOUT), BF16),
            pltpu.VMEM((2, NY // 2, NZH * EMB_ROWS, EMB), BF16),
            pltpu.VMEM((3, WOUT, LANES), BF16),
            pltpu.VMEM((2, WOUT // 2, LANES), BF16),
            pltpu.VMEM((2, WOUT, LANES), BF16),
            pltpu.VMEM((NZH * TOW_ROWS, WOUT), F32),
            pltpu.VMEM((3, TOW_ROWS, WOUT), BF16),
            pltpu.VMEM((3, TOW_ROWS, WOUT), BF16),
            pltpu.VMEM((NZH * EMB_ROWS, EMB), F32),
            pltpu.VMEM((3, EMB_ROWS, EMB), BF16),
            pltpu.VMEM((3, EMB_ROWS, EMB), BF16),
            dma((11,)),
            dma((len(SPANS),)),
            dma((len(GROUPS), 2)),
            dma((len(GROUPS), 2)),
            dma((len(GROUPS), 3)),
            dma((len(GROUPS), 3)),
            dma((len(GROUPS),)),
            dma((len(GROUPS),)),
            dma((pieces, 2, NY // 2)),
            dma((pieces, 2, NY // 2)),
            dma((10,)),
            dma((10,)),
        ],
        compiler_params=pltpu.CompilerParams(
            collective_id=0, has_side_effects=True, vmem_limit_bytes=64 * 1024 * 1024
        ),
    )(
        top_cot[0], top_pre[0], tower_pre[0], ids, lens, block_slot.reshape(1, NBLK), top_weight,
        tower_weight[0], pooled[0, :, 0, :],
    )
    outs = pl.pallas_call(
        place,
        out_shape=shapes,
        in_specs=[hbm] * 3,
        out_specs=(hbm, hbm, hbm),
        scratch_shapes=[pltpu.VMEM(s.shape, F32) for s in shapes] + [dma((2, 3))],
        compiler_params=pltpu.CompilerParams(vmem_limit_bytes=64 * 1024 * 1024),
    )(*outs)
    return outs[0], outs[1][None], outs[2].reshape(1, NBLK // (NY * NZH), BLK, EMB)


def solution(mesh):
    placed = (
        P("local", "tower", None),
        P("local", "tower", None),
        P("tower", None),
        P("local", None, "tower"),
        P("tower", None, None),
        P("local", None, "tower", None),
        P("local", None, "tower", None, None),
        P("local", None, "tower", None),
        P(),
    )
    return jax.shard_map(
        local,
        mesh=mesh,
        in_specs=placed,
        out_specs=(P("tower", "local"), P("tower", "local", None), P("tower", "local", None, None)),
        check_vma=False,
    )
```

```python
import math

import jax
import jax.numpy as jnp
from jax import lax
from jax.experimental import pallas as pl
from jax.experimental.pallas import tpu as pltpu
from jax.sharding import PartitionSpec as P

MESH = pl.DeviceIdType.MESH
F32, BF16 = jnp.float32, jnp.bfloat16

NZL, NX, NC, NY, NZH = 3, 4, 2, 8, 4
TOPW, WOUT, FEATS, EMB, BAG, FROWS, BLK = 4096, 256, 12, 128, 4, 256, 32
GROUP, SLAB, NBLK = 384, 1536, 96
SHARD = GROUP // (NZL * NX * NC)
LANES = TOPW // (NY * NZH)
PARTS = NZH
OFF = (2, 1, 3, 0)
WIDE = PARTS * LANES
AWAY = (4, 3, 5, 2, 6, 1, 7, 0)
SPANS = ((0, 1), (1, 3), (3, 5), (5, 8))
GROUPS = ((0, 0, 4), (1, 0, 4), (2, 0, 4), (3, 0, 4))
TOW_ROWS = SLAB // (NY * NZH)
EMB_ROWS = NBLK * BLK // (NY * NZH)
FACTOR = 1.0 / math.sqrt(12288)


def gelu_value(values):
    return 0.5 * values * (1.0 + lax.erf(values / math.sqrt(2.0)))


def gelu_slope(values):
    return 0.5 * (1.0 + lax.erf(values / math.sqrt(2.0))) + values * jnp.exp(
        -0.5 * values * values
    ) / math.sqrt(2.0 * math.pi)


def wide_sum(*terms):
    total = terms[0].astype(F32)
    for term in terms[1:]:
        total = total + term.astype(F32)
    return total


def kernel(
    cot_hbm, pre_hbm, tower_pre_hbm, ids_hbm, lens_hbm, slot_hbm, weight_hbm, tower_weight_hbm,
    pooled_hbm, top_hbm, tow_hbm, emb_hbm,
    out_top, out_tow, out_emb,
    cot, pre, tower_pre, ids, lens, slot, rows, weight, tower_weight, pooled, pooled_t, comp_t, slope, part, delta_t, counts, dense, slotted,
    top, tow, emb, rb_top, rb_tow, rb_emb,
    zs_top, zb_top, zf_top, zy_tow, zs_tow, zf_tow, zy_emb, zs_emb, zf_emb,
    load_sem, weight_sem, zl_send, zl_recv, x_send, x_recv, b_send, b_recv,
    y_send, y_recv, zh_send, zh_recv,
):
    t, l = lax.axis_index("tower"), lax.axis_index("local")
    core, x, zl = lax.rem(t, NC), lax.rem(lax.div(t, NC), NX), lax.div(t, NC * NX)
    y, zh = lax.div(l, NZH), lax.rem(l, NZH)

    def at_tower(zl_, x_, core_):
        return ((zl_ * NX + x_) * NC + core_, l)

    def at_local(y_, zh_):
        return (t, y_ * NZH + zh_)

    xp, xm = lax.rem(x + 1, NX), lax.rem(x + NX - 1, NX)
    xo = lax.rem(x + 2, NX)
    zl_next = [lax.rem(zl + d, NZL) for d in (1, 2)]
    zl_prev = [lax.rem(zl + NZL - d, NZL) for d in (1, 2)]
    y_next = [lax.rem(y + 1, NY), lax.rem(y + NY - 1, NY)]
    zh_next = [lax.rem(zh + 1, NZH), lax.rem(zh + NZH - 1, NZH)]
    dev_zl = [at_tower(zl_, x, core) for zl_ in zl_next]
    x_next, x_prev = (xp, xm, xo), (xm, xp, xo)
    dev_x = [at_tower(zl, x_, core) for x_ in x_next]
    dev_x_prev = [at_tower(zl, x_, core) for x_ in x_prev]
    dev_sib = at_tower(zl, x, 1 - core)
    dev_y = [at_local(y_, zh) for y_ in y_next]
    dev_zh = [at_local(y, zh_) for zh_ in zh_next + [lax.rem(zh + 2, NZH)]]

    barrier = pltpu.get_barrier_semaphore()
    peers = dev_zl + dev_x + [dev_sib] + dev_y + dev_zh

    def first_column(q, k):
        owner = lax.rem(y + k, NY) * NZH + lax.rem(zh + OFF[q], NZH)
        return pl.multiple_of(owner * LANES, LANES)

    def remote(src, dst, send, recv, device):
        return pltpu.make_async_remote_copy(
            src_ref=src, dst_ref=dst, send_sem=send, recv_sem=recv,
            device_id=device, device_id_type=MESH,
        )

    loads = [
        pltpu.make_async_copy(src, dst, load_sem.at[i])
        for i, (src, dst) in enumerate(
            [
                (cot_hbm, cot), (pre_hbm, pre), (tower_pre_hbm, tower_pre), (ids_hbm, ids),
                (lens_hbm, lens), (slot_hbm, slot), (pooled_hbm, pooled),
                (tower_weight_hbm, tower_weight),
            ]
        )
    ]
    put_top, put_tow, put_emb = [
        pltpu.make_async_copy(src, dst, load_sem.at[8 + i])
        for i, (src, dst) in enumerate(
            [(out_top, top_hbm), (out_tow, tow_hbm), (out_emb, emb_hbm)]
        )
    ]
    load_cot, load_pre, load_tower_pre, load_ids, load_lens, load_slot, load_pool, load_tw = loads
    load_cot.start()
    load_pre.start()
    for peer in peers:
        pl.semaphore_signal(barrier, inc=1, device_id=peer, device_id_type=MESH)

    def load_rest():
        load_tower_pre.start()
        load_ids.start()
        load_lens.start()
        load_pool.start()
        load_tw.start()
        load_slot.start()

    def load_weight(g):
        for j in range(*SPANS[g]):
            for q in range(PARTS):
                pltpu.make_async_copy(
                    weight_hbm.at[:, pl.ds(first_column(q, AWAY[j]), LANES)],
                    weight.at[j, :, pl.ds(q * LANES, LANES)],
                    weight_sem.at[g],
                ).start()

    def compute_delta(g):
        span, low, high = GROUPS[g]
        for j in range(*SPANS[span]):
            for q in range(low, high):
                cols = pl.ds(first_column(q, AWAY[j]), LANES)
                value = cot[:, cols].astype(F32) * gelu_slope(pre[:, cols].astype(F32))
                rows[j, zl, x, core, :, pl.ds(q * LANES, LANES)] = value.astype(BF16)

    every = slice(None)

    def group(g, zl_, x_, core_, piece=0, pieces=1):
        span, low, high = GROUPS[g]
        first, last = SPANS[span]
        wide = (high - low) * LANES // pieces
        cols = pl.ds(low * LANES + piece * wide, wide)
        return rows.at[pl.ds(first, last - first), zl_, x_, core_, :, cols]

    def zl_copy(g, d):
        here = group(g, zl, x, core)
        return remote(here, here, zl_send.at[g, d], zl_recv.at[g, d], dev_zl[d])

    def zl_arrival(g, d):
        there = group(g, zl_prev[d], x, core)
        return remote(there, there, zl_send.at[g, d], zl_recv.at[g, d], dev_zl[1 - d])

    zl_held = [zl] + zl_prev

    def x_copy(g, e, d):
        here = group(g, zl_held[e], x, core)
        return remote(here, here, x_send.at[g, e, d], x_recv.at[g, e, d], dev_x[d])

    def x_arrival(g, e, d):
        there = group(g, zl_held[e], x_prev[d], core)
        return remote(there, there, x_send.at[g, e, d], x_recv.at[g, e, d], dev_x_prev[d])

    def b_copy(g):
        here = group(g, every, every, core)
        return remote(here, here, b_send.at[g], b_recv.at[g], dev_sib)

    def b_arrival(g):
        there = group(g, every, every, 1 - core)
        return remote(there, there, b_send.at[g], b_recv.at[g], dev_sib)

    def step_z(g):
        for d in range(2):
            zl_copy(g, d).start()
        for d in range(3):
            x_copy(g, 0, d).start()

    def step_x(g):
        for e in range(1, NZL):
            zl_arrival(g, e - 1).wait_recv()
            for d in range(3):
                x_copy(g, e, d).start()

    def step_b(g):
        for e in range(NZL):
            for d in range(3):
                x_arrival(g, e, d).wait_recv()
        b_copy(g).start()

    half_rows = [WOUT // 2] * PARTS + [NZH * TOW_ROWS // 2, NZH * EMB_ROWS // 2]

    def chunk(p, k):
        if p < PARTS:
            return top.at[p, k]
        y_ = lax.rem(y + k, NY)
        if p == PARTS:
            return tow.at[pl.ds(pl.multiple_of(y_ * (NZH * TOW_ROWS), 16), NZH * TOW_ROWS)]
        return emb.at[pl.ds(pl.multiple_of(y_ * (NZH * EMB_ROWS), 16), NZH * EMB_ROWS)]

    def landing(p, d, h):
        ref = rb_top.at[p, d, h] if p < PARTS else (rb_tow, rb_emb)[p - PARTS].at[d, h]
        return ref.at[pl.ds(0, half_rows[p])] if h == 0 else ref

    def half(p, d):
        return pl.ds(d * half_rows[p], half_rows[p])

    def y_copy(p, d, h):
        if h == 0:
            src = chunk(p, NY // 2).at[half(p, d)]
        else:
            src = chunk(p, NY // 2 - h if d == 0 else NY // 2 + h)
        return remote(src, landing(p, d, h), y_send.at[p, d, h], y_recv.at[p, d, h], dev_y[d])

    def step_s(p):
        for d in range(2):
            y_copy(p, d, 0).start()

    def step_h(p, h, d):
        y_copy(p, d, h - 1).wait_recv()
        own = chunk(p, NY // 2 - h if d == 0 else NY // 2 + h)
        if h == 1:
            own = own.at[half(p, d)]
        own[...] = wide_sum(own[...], landing(p, d, h - 1)[...]).astype(BF16)
        y_copy(p, d, h).start()

    def y_total(p):
        last = NY // 2 - 1
        for d in range(2):
            y_copy(p, d, last).wait_recv()
        return wide_sum(chunk(p, 0)[...], landing(p, 0, last)[...], landing(p, 1, last)[...])

    def zh_copy(i, src, dst, d):
        return remote(src, dst, zh_send.at[i], zh_recv.at[i], dev_zh[d])

    top_halves = [pl.ds(d * (WOUT // 2), WOUT // 2) for d in range(2)]
    zc_top = [zh_copy(d, zs_top.at[0, top_halves[d]], zb_top.at[d], d) for d in range(2)]
    zc_top += [zh_copy(2 + d, zs_top.at[1 + d], zf_top.at[d], d) for d in range(2)]
    zc_tow = [zh_copy(4 + d, zs_tow.at[d], zf_tow.at[d], d) for d in range(3)]
    zc_emb = [zh_copy(7 + d, zs_emb.at[d], zf_emb.at[d], d) for d in range(3)]

    def step_f_top(q):
        total = y_total(q)
        if q == 0:
            zs_top[0] = total.astype(BF16)
            for d in range(2):
                zc_top[d].start()
        elif q < 3:
            d = q - 1
            zc_top[d].wait_recv()
            zs_top[q] = total.astype(BF16)
            zs_top[q, top_halves[d]] = wide_sum(
                total[d * (WOUT // 2) : (d + 1) * (WOUT // 2)], zb_top[d]
            ).astype(BF16)
            zc_top[q + 1].start()
        else:
            out_top[...] = total

    def blocks(ref, size, offset):
        first = lax.rem(zh + offset, NZH) * size
        return ref[pl.ds(pl.multiple_of(first, 16), size), :]

    def step_f_pair(p, zy, zs, size, copies):
        zy[...] = y_total(p)
        for d in (2, 0, 1):
            zs[d] = blocks(zy, size, (1, 3, 2)[d]).astype(BF16)
            copies[d].start()

    def finish_pair(out, zy, zf, size, copies):
        for d in range(3):
            copies[d].wait_recv()
        out[...] = wide_sum(blocks(zy, size, 0), zf[0], zf[1], zf[2])

    def prepare_pre():
        load_tower_pre.wait()
        values = tower_pre[...].astype(F32)
        slope[...] = gelu_slope(values)
        comp_t[...] = gelu_value(values).T.astype(BF16)

    def prepare_counts(first, last):
        size = 64
        if first == 0:
            load_ids.wait()
            load_lens.wait()

        def feature(f, carry):
            length = lens[f]
            masked = [jnp.where(j < length, ids[f, j : j + 1, :], -1) for j in range(BAG)]
            for part_ in range(FROWS // size):
                table = lax.broadcasted_iota(jnp.int32, (size, GROUP), 0) + part_ * size
                hits = [jnp.where(m == table, 1.0, 0.0) for m in masked]
                count = (hits[0] + hits[1]) + (hits[2] + hits[3])
                counts[f, pl.ds(part_ * size, size), :] = count.astype(BF16)
            return carry

        lax.fori_loop(first, last, feature, 0)

    def prepare_pooled(first, last):
        if first == 0:
            load_pool.wait()
        for c in range(first, last):
            block = pooled[:, c * EMB : (c + 1) * EMB].astype(F32)
            pooled_t[c * EMB : (c + 1) * EMB, :] = block.T.astype(BF16)

    def compute_top(g):
        span, low, high = GROUPS[g]
        for j in range(*SPANS[span]):
            deltas = rows[j, :, :, :, :, low * LANES : high * LANES].reshape(GROUP, (high - low) * LANES)
            term = (jnp.dot(comp_t[...], deltas, preferred_element_type=F32) * FACTOR).astype(BF16)
            for q in range(low, high):
                value = term[:, (q - low) * LANES : (q - low + 1) * LANES]
                top[q, AWAY[j]] = value

    def compute_part(i):
        first, last = SPANS[i]
        loaded = weight.at[pl.ds(first, last - first)]
        pltpu.make_async_copy(loaded, loaded, weight_sem.at[i]).wait()
        for j in range(first, last):
            product = lax.dot_general(
                rows[j].reshape(GROUP, WIDE), weight[j],
                (((1,), (1,)), ((), ())), preferred_element_type=F32,
            )
            part[...] = product if j == 0 else part[...] + product

    def compute_tow():
        feature_grad = part[...].astype(BF16).astype(F32)
        delta_t[...] = (feature_grad * slope[...]).astype(BF16)
        for k in AWAY:
            first = lax.rem(y + k, NY) * (NZH * TOW_ROWS)
            here = pl.ds(pl.multiple_of(first, 16), NZH * TOW_ROWS)
            term = jnp.dot(pooled_t[here, :], delta_t[...], preferred_element_type=F32)
            tow[here, :] = (term * FACTOR).astype(BF16)
            if k == NY // 2:
                step_s(PARTS)

    def compute_emb():
        load_tw.wait()
        for f in range(FEATS):
            grad = lax.dot_general(
                delta_t[...], tower_weight[f * EMB : (f + 1) * EMB, :],
                (((1,), (1,)), ((), ())), preferred_element_type=F32,
            ).astype(BF16)
            dense[f * FROWS : (f + 1) * FROWS, :] = jnp.dot(
                counts[f], grad, preferred_element_type=F32
            )
        load_slot.wait()
        numbers = lax.broadcasted_iota(jnp.int32, (NBLK, NBLK), 0)
        moves = jnp.where(slot[...] == numbers, 1.0, 0.0).astype(BF16)
        for i in range(0, BLK, 2):
            taken = [dense[pl.ds(i + j, NBLK, stride=BLK), :].astype(BF16) for j in range(2)]
            moved = jnp.dot(moves, jnp.concatenate(taken, 1), preferred_element_type=F32)
            for j in range(2):
                slotted[pl.ds(i + j, NBLK, stride=BLK), :] = moved[:, j * EMB : (j + 1) * EMB]
        for k in AWAY:
            first = lax.rem(y + k, NY) * (NZH * EMB_ROWS)
            here = pl.ds(pl.multiple_of(first, 16), NZH * EMB_ROWS)
            emb[here, :] = slotted[here, :].astype(BF16)
            if k == NY // 2:
                step_s(PARTS + 1)

    load_cot.wait()
    load_pre.wait()
    compute_delta(0)
    pl.semaphore_wait(barrier, len(peers))
    step_z(0)
    compute_delta(1)
    step_z(1)
    compute_delta(2)
    step_z(2)
    compute_delta(3)
    step_z(3)
    load_rest()
    prepare_pre()
    prepare_counts(0, 4)
    step_x(0)
    step_x(1)
    step_x(2)
    step_b(0)
    step_x(3)
    load_weight(0)
    load_weight(1)
    b_arrival(0).wait_recv()
    compute_top(0)
    for p in range(PARTS):
        step_s(p)
    step_b(1)
    prepare_counts(4, 8)
    b_arrival(1).wait_recv()
    compute_top(1)
    step_h(0, 1, 0)
    step_h(0, 1, 1)
    step_h(1, 1, 0)
    step_h(1, 1, 1)
    step_h(2, 1, 0)
    step_h(2, 1, 1)
    step_h(3, 1, 0)
    step_h(3, 1, 1)
    step_b(2)
    load_weight(2)
    load_weight(3)
    compute_part(0)
    compute_part(1)
    prepare_pooled(0, 6)
    b_arrival(2).wait_recv()
    compute_top(2)
    step_b(3)
    step_h(0, 2, 0)
    step_h(0, 2, 1)
    step_h(1, 2, 0)
    step_h(1, 2, 1)
    compute_part(2)
    prepare_pooled(6, 12)
    step_h(2, 2, 0)
    step_h(2, 2, 1)
    step_h(3, 2, 0)
    step_h(3, 2, 1)
    prepare_counts(8, 12)
    b_arrival(3).wait_recv()
    compute_part(3)
    compute_tow()
    compute_top(3)
    step_h(0, 3, 0)
    step_h(0, 3, 1)
    step_h(1, 3, 0)
    step_h(1, 3, 1)
    compute_emb()
    step_h(4, 1, 0)
    step_h(4, 1, 1)
    step_h(2, 3, 0)
    step_h(2, 3, 1)
    step_f_top(0)
    step_h(5, 1, 0)
    step_h(5, 1, 1)
    step_h(4, 2, 0)
    step_h(4, 2, 1)
    step_f_top(1)
    step_h(5, 2, 0)
    step_h(5, 2, 1)
    step_f_top(2)
    step_h(4, 3, 0)
    step_h(4, 3, 1)
    step_h(5, 3, 0)
    step_h(5, 3, 1)
    step_h(3, 3, 0)
    step_h(3, 3, 1)
    step_f_pair(PARTS, zy_tow, zs_tow, TOW_ROWS, zc_tow)
    step_f_pair(PARTS + 1, zy_emb, zs_emb, EMB_ROWS, zc_emb)
    step_f_top(3)
    for d in range(2):
        zc_top[2 + d].wait_recv()
    out_top[...] = wide_sum(out_top[...], zf_top[0], zf_top[1])
    put_top.start()
    finish_pair(out_tow, zy_tow, zf_tow, TOW_ROWS, zc_tow)
    put_tow.start()
    finish_pair(out_emb, zy_emb, zf_emb, EMB_ROWS, zc_emb)
    put_emb.start()

    put_top.wait()
    put_tow.wait()
    put_emb.wait()
    for g in range(len(GROUPS)):
        for d in range(2):
            zl_copy(g, d).wait_send()
        for e in range(NZL):
            for d in range(3):
                x_copy(g, e, d).wait_send()
        b_copy(g).wait_send()
    for p in range(PARTS + 2):
        for d in range(2):
            for h in range(NY // 2):
                y_copy(p, d, h).wait_send()
    for copy in zc_top + zc_tow + zc_emb:
        copy.wait_send()


def place(*refs):
    sources, results, held, sems = refs[:3], refs[3:6], refs[6:9], refs[9]
    first = [pltpu.make_async_copy(*two, sems.at[0, i]) for i, two in enumerate(zip(sources, held))]
    second = [pltpu.make_async_copy(*two, sems.at[1, i]) for i, two in enumerate(zip(held, results))]
    for copy in first:
        copy.start()
    for one, two in zip(first, second):
        one.wait()
        two.start()
    for copy in second:
        copy.wait()


def local(
    top_cot, top_pre, top_weight, tower_pre, tower_weight, pooled, feature_ids, bag_lengths, block_slot
):
    ids = jnp.transpose(feature_ids[0, :, 0], (1, 2, 0))
    lens = jnp.transpose(bag_lengths[0], (2, 1, 0))
    hbm = pl.BlockSpec(memory_space=pltpu.HBM)
    dma = pltpu.SemaphoreType.DMA
    pieces = PARTS + 2
    shapes = (
        jax.ShapeDtypeStruct((WOUT, LANES), F32),
        jax.ShapeDtypeStruct((TOW_ROWS, WOUT), F32),
        jax.ShapeDtypeStruct((EMB_ROWS, EMB), F32),
    )
    outs = pl.pallas_call(
        kernel,
        out_shape=shapes,
        in_specs=[hbm] * 9,
        out_specs=(hbm, hbm, hbm),
        scratch_shapes=[pltpu.VMEM(s.shape, F32) for s in shapes]
        + [
            pltpu.VMEM((SHARD, TOPW), BF16),
            pltpu.VMEM((SHARD, TOPW), BF16),
            pltpu.VMEM((GROUP, WOUT), BF16),
            pltpu.VMEM((FEATS, BAG, GROUP), jnp.int32),
            pltpu.VMEM((FEATS, 1, GROUP), jnp.int32),
            pltpu.VMEM((1, NBLK), jnp.int32),
            pltpu.VMEM((NY, NZL, NX, NC, SHARD, WIDE), BF16),
            pltpu.VMEM((NY, WOUT, WIDE), BF16),
            pltpu.VMEM((SLAB, WOUT), BF16),
            pltpu.VMEM((GROUP, SLAB), BF16),
            pltpu.VMEM((SLAB, GROUP), BF16),
            pltpu.VMEM((WOUT, GROUP), BF16),
            pltpu.VMEM((GROUP, WOUT), F32),
            pltpu.VMEM((GROUP, WOUT), F32),
            pltpu.VMEM((GROUP, WOUT), BF16),
            pltpu.VMEM((FEATS, FROWS, GROUP), BF16),
            pltpu.VMEM((FEATS * FROWS, EMB), F32),
            pltpu.VMEM((NBLK * BLK, EMB), F32),
            pltpu.VMEM((PARTS, NY, WOUT, LANES), BF16),
            pltpu.VMEM((SLAB, WOUT), BF16),
            pltpu.VMEM((NBLK * BLK, EMB), BF16),
            pltpu.VMEM((PARTS, 2, NY // 2, WOUT, LANES), BF16),
            pltpu.VMEM((2, NY // 2, NZH * TOW_ROWS, WOUT), BF16),
            pltpu.VMEM((2, NY // 2, NZH * EMB_ROWS, EMB), BF16),
            pltpu.VMEM((3, WOUT, LANES), BF16),
            pltpu.VMEM((2, WOUT // 2, LANES), BF16),
            pltpu.VMEM((2, WOUT, LANES), BF16),
            pltpu.VMEM((NZH * TOW_ROWS, WOUT), F32),
            pltpu.VMEM((3, TOW_ROWS, WOUT), BF16),
            pltpu.VMEM((3, TOW_ROWS, WOUT), BF16),
            pltpu.VMEM((NZH * EMB_ROWS, EMB), F32),
            pltpu.VMEM((3, EMB_ROWS, EMB), BF16),
            pltpu.VMEM((3, EMB_ROWS, EMB), BF16),
            dma((11,)),
            dma((len(SPANS),)),
            dma((len(GROUPS), 2)),
            dma((len(GROUPS), 2)),
            dma((len(GROUPS), NZL, 3)),
            dma((len(GROUPS), NZL, 3)),
            dma((len(GROUPS),)),
            dma((len(GROUPS),)),
            dma((pieces, 2, NY // 2)),
            dma((pieces, 2, NY // 2)),
            dma((10,)),
            dma((10,)),
        ],
        compiler_params=pltpu.CompilerParams(
            collective_id=0, has_side_effects=True, vmem_limit_bytes=64 * 1024 * 1024
        ),
    )(
        top_cot[0], top_pre[0], tower_pre[0], ids, lens, block_slot.reshape(1, NBLK), top_weight,
        tower_weight[0], pooled[0, :, 0, :],
    )
    outs = pl.pallas_call(
        place,
        out_shape=shapes,
        in_specs=[hbm] * 3,
        out_specs=(hbm, hbm, hbm),
        scratch_shapes=[pltpu.VMEM(s.shape, F32) for s in shapes] + [dma((2, 3))],
        compiler_params=pltpu.CompilerParams(vmem_limit_bytes=64 * 1024 * 1024),
    )(*outs)
    return outs[0], outs[1][None], outs[2].reshape(1, NBLK // (NY * NZH), BLK, EMB)


def solution(mesh):
    placed = (
        P("local", "tower", None),
        P("local", "tower", None),
        P("tower", None),
        P("local", None, "tower"),
        P("tower", None, None),
        P("local", None, "tower", None),
        P("local", None, "tower", None, None),
        P("local", None, "tower", None),
        P(),
    )
    return jax.shard_map(
        local,
        mesh=mesh,
        in_specs=placed,
        out_specs=(P("tower", "local"), P("tower", "local", None), P("tower", "local", None, None)),
        check_vma=False,
    )
```
